256 devices in a mesh: seq: 32 (over z, x), tp: 8 (over y, core).
Axes of the slice: x: 4, y: 4, z: 8, core: 2. Of those that a mesh axis runs over, the one named last changes fastest.
Arguments:
- x_in: bfloat16 [8192, 16384], P('seq', 'tp'), may hold values from -6 to 6
- bc_in: bfloat16 [8192, 8, 512], P('seq', 'tp'), may hold values from -6 to 6
- gate_in: bfloat16 [8192, 16384], P('seq', 'tp'), may hold values from -6 to 6
- dt_raw: float32 [8192, 256], P('seq', 'tp'), may hold values from -5 to 2
- decay_rate: float32 [256], P('tp'), may hold values from 0 to 2, as said below
- skip_gain: float32 [256], P('tp'), may hold values from 0.5 to 1.5
- conv_x: float32 [4, 16384], P(None, 'tp'), may hold values from -3 to 3
- conv_bc: float32 [4, 8, 512], P(None, 'tp'), may hold values from -3 to 3
- norm_gain: float32 [16384], P('tp'), may hold values from 0.1 to 1.9
- out_weight: bfloat16 [16384, 4096], P('tp', 'seq'), may hold values from -0.09375 to 0.09375
- lengths: int32 [4], replicated, may hold values from 1 to 4096, as said below
Outputs:
- mixed: bfloat16 [8192, 4096], P('seq', 'tp')
The draws below stay inside these ranges and needn't reach their ends.
Inputs may be any that keep to these rules, and one draw needn't show every extreme that they name: The lengths sum to 8192; the second is exactly 4096 and the first is more than 256 and at most 2048. `decay_rate`: positive.
All inputs are finite; a program needn't handle non-finite values.
Results may differ from the reference program's by a relative error of at most 0.02.
Values may be sent and summed in bfloat16 or wider, within the bound.
No kernel may reach another device: no remote copies, remote signals or barrier semaphores. Data moves between devices by JAX's collectives and lax.ppermute only.
A program may use at most 192 MiB of HBM per device.

```python
import math
import jax
import jax.numpy as jnp
from jax import lax

INNER = 16384
RECURRENT_HEADS = 256
HEAD_DIM = 64
STATE = 256
GROUPS = 8
DIM = 4096
CONV = 4
SPAN = 256
ROWS_DEV = 256
TOKEN_SLOTS = 8192
N_TP = 8


def draw_decay_rate(key, part):
    key = jax.random.fold_in(key, 7)
    key_rank, key_fast, key_slow = jax.random.split(key, 3)
    fast_count = RECURRENT_HEADS // 2
    fast_lo = 0.05
    fast_hi = 1.0
    slow_lo = 0.5
    slow_hi = 2.5
    ranking = jax.random.permutation(key_rank, RECURRENT_HEADS)
    fast = ranking < fast_count
    fast_rate = jnp.exp(jax.random.uniform(key_fast, (RECURRENT_HEADS,), jnp.float32, math.log(fast_lo), math.log(fast_hi)))
    slow_rate = jnp.exp(jax.random.uniform(key_slow, (RECURRENT_HEADS,), jnp.float32, math.log(slow_lo), math.log(slow_hi))) * (20.0 / TOKEN_SLOTS)
    return jnp.where(fast, fast_rate, slow_rate).astype(jnp.float32)


def draw_dt_raw(key, part):
    key = jax.random.fold_in(key, 13)
    block_random_key, noise_random_key, spike_random_key, spike_value_key = jax.random.split(key, 4)
    low_end = -4.5
    high_end = -2.5
    jitter_width = 0.5
    block_count = TOKEN_SLOTS // SPAN
    block_level = jax.random.uniform(block_random_key, (block_count, 1, 1), jnp.float32, low_end, high_end)
    jitter = jax.random.uniform(noise_random_key, (block_count, SPAN, RECURRENT_HEADS), jnp.float32, -jitter_width, jitter_width)
    value_baseline = (block_level + jitter).reshape(TOKEN_SLOTS, RECURRENT_HEADS)
    spike_rows = jax.random.bernoulli(spike_random_key, 1.0 / 256.0, (TOKEN_SLOTS, 1))
    spike_value = jax.random.uniform(spike_value_key, (TOKEN_SLOTS, RECURRENT_HEADS), jnp.float32, -0.5, 1.0)
    return jnp.where(spike_rows, spike_value, value_baseline).astype(jnp.float32)


def draw_lengths(key, part):
    key = jax.random.fold_in(key, 21)
    key_lead, key_split = jax.random.split(key, 2)
    half_total = TOKEN_SLOTS // 2
    quarter_total = TOKEN_SLOTS // 4
    leading = jax.random.randint(key_lead, (), ROWS_DEV + 1, quarter_total + 1, dtype=jnp.int32)
    remaining = half_total - leading
    middle_len = jax.random.randint(key_split, (), 1, remaining, dtype=jnp.int32)
    return jnp.stack([leading, jnp.int32(half_total) + 0 * leading, middle_len, remaining - middle_len]).astype(jnp.int32)


def spiked(values, stream_key, source, target, shards_of, factor):
    owner, partner = [(jnp.arange(values.shape[position]) // (values.shape[position] // shards_of)).reshape([-1 if axis == position else 1 for axis in range(values.ndim)]) for position in (source, target)]
    chosen = jax.random.permutation(stream_key, shards_of)[partner]
    strong = (owner == chosen) | (owner == (partner + shards_of // 2) % shards_of)
    return jnp.where(strong, factor * values, values)


def shard_levels(rng, extent, cuts, low, largest):
    loudness, own = 1.0, jax.random.fold_in(rng, 6)
    for dim, blocks in cuts:
        heights = jnp.exp(jax.random.uniform(jax.random.fold_in(own, dim), (blocks,), jnp.float32, low / len(cuts), largest / len(cuts)))
        loudness = loudness * jnp.repeat(heights, extent[dim] // blocks).reshape([-1 if axis == dim else 1 for axis in range(len(extent))])
    return loudness


def normal_values(key, shape, scale, most, cuts=(), kind=jnp.bfloat16):
    level = shard_levels(key, shape, cuts, -0.22, 0.18) if cuts else 1.0
    values = jax.random.normal(key, shape, jnp.float32) * scale * level
    return jnp.minimum(jnp.maximum(values, -most), most).astype(kind)


def gaussian_with(own_key, dims, scale, limit, cuts, heavy, kind=jnp.bfloat16):
    values = scale * jax.random.normal(own_key, dims, jnp.float32)
    if cuts:
        values = values * shard_levels(own_key, dims, cuts, -0.22, 0.18)
    return jnp.clip(spiked(values, jax.random.fold_in(own_key, 3), *heavy), -limit, limit).astype(kind)


def setup_inputs(seed: int = 0) -> dict:
    keys = jax.random.split(jax.random.key(seed), 12)
    return {
        "x_in": normal_values(keys[0], (TOKEN_SLOTS, INNER), 1.0, 6.0, ((0, 32), (1, 8))),
        "bc_in": normal_values(keys[1], (TOKEN_SLOTS, GROUPS, 2 * STATE), 1.0, 6.0, ((0, 32), (1, 8))),
        "gate_in": normal_values(keys[2], (TOKEN_SLOTS, INNER), 1.0, 6.0, ((0, 32), (1, 8))),
        "dt_raw": draw_dt_raw(jax.random.fold_in(keys[11], 71), 0),
        "decay_rate": draw_decay_rate(jax.random.fold_in(keys[11], 71), 0),
        "skip_gain": jnp.clip(0.5 + 1.0 * jax.random.uniform(keys[5], (RECURRENT_HEADS,), jnp.float32) ** shard_levels(keys[5], (RECURRENT_HEADS,), ((0, 8),), -0.2, 0.2), 0.5, 1.5),
        "conv_x": normal_values(keys[6], (CONV, INNER), CONV ** -0.5, 3.0, ((1, 8),), jnp.float32),
        "conv_bc": normal_values(keys[7], (CONV, GROUPS, 2 * STATE), CONV ** -0.5, 3.0, ((1, 8),), jnp.float32),
        "norm_gain": jnp.clip(1.0 + 0.18 * jax.random.normal(keys[8], (INNER,), jnp.float32), 0.1, 1.9),
        "out_weight": gaussian_with(keys[9], (INNER, DIM), INNER ** -0.5, 0.09375, ((0, 8), (1, 32)), (0, 1, 32, 2.75)),
        "lengths": draw_lengths(jax.random.fold_in(keys[11], 71), 0),
    }


def reference(x_in, bc_in, gate_in, dt_raw, decay_rate, skip_gain, conv_x, conv_bc, norm_gain, out_weight, lengths):
    per_group = RECURRENT_HEADS // GROUPS
    starts = (jnp.cumsum(lengths) - lengths).astype(jnp.int32)
    places = jnp.arange(TOKEN_SLOTS, dtype=jnp.int32)
    first = lax.optimization_barrier(jnp.max(jnp.where(starts[None, :] <= places[:, None], starts[None, :], 0), axis=1)).astype(jnp.int32)
    step_size = jax.nn.softplus(dt_raw)
    rate = -decay_rate[None, :] * step_size
    padded_x = jnp.concatenate([jnp.zeros((CONV - 1, INNER), jnp.bfloat16), x_in], axis=0)
    padded_bc = jnp.concatenate([jnp.zeros((CONV - 1, GROUPS, 2 * STATE), jnp.bfloat16), bc_in], axis=0)
    highest = lax.Precision.HIGHEST

    def block_step(carry, index):
        base_offset = (index * SPAN).astype(jnp.int32)
        window_x = lax.dynamic_slice_in_dim(padded_x, base_offset, SPAN + CONV - 1, 0)
        window_bc = lax.dynamic_slice_in_dim(padded_bc, base_offset, SPAN + CONV - 1, 0)
        place_b = base_offset + jnp.arange(SPAN, dtype=jnp.int32)
        first_b = lax.dynamic_slice_in_dim(first, base_offset, SPAN, 0)
        acc_x = jnp.zeros((SPAN, INNER), jnp.float32)
        acc_bc = jnp.zeros((SPAN, GROUPS, 2 * STATE), jnp.float32)
        for offset in range(CONV):
            usable = place_b - CONV + 1 + offset >= first_b
            acc_x = acc_x + jnp.where(usable[:, None], conv_x[offset][None, :] * window_x[offset:offset + SPAN].astype(jnp.float32), 0.0)
            acc_bc = acc_bc + jnp.where(usable[:, None, None], conv_bc[offset][None] * window_bc[offset:offset + SPAN].astype(jnp.float32), 0.0)
        conv_out = jax.nn.silu(acc_x).astype(jnp.bfloat16)
        bc_out = jax.nn.silu(acc_bc).astype(jnp.bfloat16)
        keys_b = bc_out[:, :, :STATE].astype(jnp.float32)
        query_c = bc_out[:, :, STATE:].astype(jnp.float32)
        xheads = conv_out.reshape(SPAN, GROUPS, per_group, HEAD_DIM).astype(jnp.float32)
        rate_b = lax.dynamic_slice_in_dim(rate, base_offset, SPAN, 0)
        step_b = lax.dynamic_slice_in_dim(step_size, base_offset, SPAN, 0)
        logdec = jnp.cumsum(rate_b, axis=0)
        intersection = jnp.einsum('qgn,sgn->gqs', query_c, keys_b, precision=highest)
        causal = (place_b[None, :] <= place_b[:, None]) & (place_b[None, :] >= first_b[:, None])
        log_t = logdec.T
        spread = jnp.exp(jnp.where(causal[None], log_t[:, :, None] - log_t[:, None, :], -jnp.inf)) * step_b.T[:, None, :]
        mixing = (intersection[:, None] * spread.reshape(GROUPS, per_group, SPAN, SPAN)).astype(jnp.bfloat16)
        within = jnp.einsum('gjqs,sgjp->qgjp', mixing.astype(jnp.float32), xheads, precision=highest)
        log_end = logdec[-1]
        first_end = first_b[-1]
        keep = place_b >= first_end
        weight_u = jnp.where(keep[:, None], jnp.exp(log_end[None, :] - logdec) * step_b, 0.0)
        inputs_u = (weight_u.reshape(SPAN, GROUPS, per_group)[..., None] * xheads).astype(jnp.bfloat16)
        local_state = jnp.einsum('qgjp,qgn->gjpn', inputs_u.astype(jnp.float32), keys_b, precision=highest)
        carried = (jnp.exp(log_end) * (first_end <= base_offset - 1).astype(jnp.float32)).reshape(GROUPS, per_group)
        reach = jnp.exp(logdec) * (first_b <= base_offset - 1).astype(jnp.float32)[:, None]
        across = jnp.einsum('qgn,gjpn->qgjp', query_c, carry, precision=highest)
        across = across * reach.reshape(SPAN, GROUPS, per_group)[..., None]
        output = within + across + skip_gain.reshape(GROUPS, per_group)[None, :, :, None] * xheads
        gate_b = lax.dynamic_slice_in_dim(gate_in, base_offset, SPAN, 0).astype(jnp.float32)
        gated = output.reshape(SPAN, INNER) * jax.nn.silu(gate_b)
        grouped = gated.reshape(SPAN, GROUPS, INNER // GROUPS)
        scale = lax.rsqrt(lax.optimization_barrier(jnp.mean(grouped * grouped, axis=-1, keepdims=True)) + 1e-05)
        normed = ((grouped * scale).reshape(SPAN, INNER) * norm_gain[None, :]).astype(jnp.bfloat16)
        new_carry = carried[..., None, None] * carry + local_state
        return (new_carry, normed)
    start_state = jnp.zeros((GROUPS, per_group, HEAD_DIM, STATE), jnp.float32)
    final_state, normed_blocks = lax.scan(block_step, start_state, jnp.arange(TOKEN_SLOTS // SPAN, dtype=jnp.int32))
    normed_all = normed_blocks.reshape(TOKEN_SLOTS, INNER)
    width = INNER // N_TP
    total = jnp.zeros((TOKEN_SLOTS, DIM), jnp.float32)
    for index in range(N_TP):
        part_sum = jnp.dot(normed_all[:, index * width:(index + 1) * width], out_weight[index * width:(index + 1) * width], preferred_element_type=jnp.float32)
        rounded = lax.optimization_barrier(part_sum.astype(jnp.bfloat16))
        total = total + rounded.astype(jnp.float32)
    return total.astype(jnp.bfloat16)
```

```python
import functools

import jax
import jax.numpy as jnp
from jax import lax
from jax.experimental import pallas as pl
from jax.experimental.pallas import tpu as pltpu
from jax.sharding import Mesh, PartitionSpec as P

SPAN = 256
NX = 4
NY = 4
HEADS = 8
HEAD_DIM = 64
WIDTH = HEADS * HEAD_DIM
STATE = 256
BC = 2 * STATE
PAY = WIDTH + BC + 128
F32 = jnp.float32
BF16 = jnp.bfloat16
VMEM = pl.BlockSpec(memory_space=pltpu.VMEM)
SMEM = pl.BlockSpec(memory_space=pltpu.SMEM)
PARAMS = pltpu.CompilerParams(vmem_limit_bytes=48 * 1024 * 1024)


def call(kernel, scalars, args, outs, scratch=(), flops=0, nbytes=0):
    return pl.pallas_call(
        kernel,
        in_specs=[SMEM] + [VMEM] * len(args),
        out_specs=tuple(VMEM for _ in outs),
        out_shape=tuple(jax.ShapeDtypeStruct(s, d) for s, d in outs),
        scratch_shapes=list(scratch),
        compiler_params=PARAMS,
        cost_estimate=pl.CostEstimate(flops=flops, bytes_accessed=nbytes, transcendentals=0),
    )(scalars, *args)


def shift(v, axis, by):
    n = lax.axis_size(axis)
    return lax.ppermute(v, axis, [(i, (i + by) % n) for i in range(n)])


def around(v, by):
    return lax.rem(v + by, 4)


def sigmoid(v):
    return 0.5 * jnp.tanh(0.5 * v) + 0.5


def lanes(q, width):
    return pl.ds(pl.multiple_of(q * width, width), width)


def pack_kernel(sc, x_ref, bc_ref, dt_ref, own, to_next, to_prev, to_far, h0, h1, h2, h3, dts):
    x = sc[0]
    dts[...] = jnp.zeros_like(dts)
    dts[:, : 4 * HEADS] = dt_ref[...]
    raw = dts[...]
    lane = lax.broadcasted_iota(jnp.int32, raw.shape, 1)
    for by, out in ((0, own), (1, to_next), (3, to_prev), (2, to_far)):
        q = around(x, by)
        out[:, :WIDTH] = x_ref[:, lanes(q, WIDTH)]
        out[:, WIDTH : WIDTH + BC] = bc_ref[...]
        mine = pltpu.roll(raw, lax.rem(128 - HEADS * q, 128), 1)
        mine = jnp.where(lane < HEADS, mine, 0.0)
        hi = mine.astype(BF16).astype(F32)
        mid = (mine - hi).astype(BF16).astype(F32)
        low = (mine - hi - mid).astype(BF16).astype(F32)
        out[:, WIDTH + BC :] = (
            hi + pltpu.roll(mid, HEADS, 1) + pltpu.roll(low, 2 * HEADS, 1)
        ).astype(BF16)
    for q, out in enumerate((h0, h1, h2, h3)):
        out[:, :WIDTH] = x_ref[SPAN - 16 :, q * WIDTH : (q + 1) * WIDTH]
        out[:, WIDTH:] = bc_ref[SPAN - 16 :, :]


def split_kernel(sc, g_ref, own, to_next, to_prev, to_far):
    x = sc[0]
    for by, out in ((0, own), (1, to_next), (3, to_prev), (2, to_far)):
        out[...] = g_ref[:, lanes(around(x, by), WIDTH)]


def block_kernel(
    sc, own, prev, nxt, far, h0, h1, h2, h3, cw_ref, cbw_ref, skip_ref, decay_ref,
    y_out, c_out, re_out, t_out,
    pay, ext, conv, gram, carry, weighted,
):
    x = sc[0]
    base = sc[1] * (NX * SPAN)
    s1, s2, s3 = sc[4], sc[5], sc[6]
    pay[x] = own[...]
    pay[around(x, 3)] = prev[...]
    pay[around(x, 1)] = nxt[...]
    pay[around(x, 2)] = far[...]
    ext[0:8] = (
        h0[8:16].astype(F32) + h1[8:16].astype(F32) + h2[8:16].astype(F32) + h3[8:16].astype(F32)
    )
    carry[...] = jnp.zeros_like(carry)
    taps_x = cw_ref[:, lanes(x, WIDTH)]
    taps_bc = cbw_ref[...]
    decay = decay_ref[...]

    def first_of(t):
        return jnp.where(t >= s3, s3, jnp.where(t >= s2, s2, jnp.where(t >= s1, s1, 0)))

    def turn(j, before):
        start = base + j * SPAN

        @pl.when(j > 0)
        def _():
            ext[0:8] = ext[SPAN : SPAN + 8]

        ext[8:] = pay[j][:, : WIDTH + BC].astype(F32)
        row = lax.broadcasted_iota(jnp.int32, (SPAN, 128), 0)
        lane = lax.broadcasted_iota(jnp.int32, (SPAN, 128), 1)
        lane1 = lax.broadcasted_iota(jnp.int32, (1, 128), 1)
        place = start + row
        first = first_of(place)
        pos = place - first
        for part in range((WIDTH + BC) // 128):
            cols = slice(part * 128, part * 128 + 128)
            taps, at = (taps_x, part * 128) if part * 128 < WIDTH else (taps_bc, part * 128 - WIDTH)
            acc = taps[3:4, at : at + 128] * ext[8 : 8 + SPAN, cols]
            for back in (1, 2, 3):
                term = taps[3 - back : 4 - back, at : at + 128] * ext[8 - back : 8 - back + SPAN, cols]
                acc = acc + jnp.where(pos >= back, term, 0.0)
            conv[:, cols] = (acc * sigmoid(acc)).astype(BF16)
        keys = conv[:, WIDTH : WIDTH + STATE]
        query = conv[:, WIDTH + STATE :]
        packed = pay[j][:, WIDTH + BC :].astype(F32)
        raw = packed + pltpu.roll(packed, 128 - HEADS, 1) + pltpu.roll(packed, 128 - 2 * HEADS, 1)
        step = jnp.maximum(raw, 0.0) + jnp.log1p(jnp.exp(-jnp.abs(raw)))
        rate = jnp.where(lane < HEADS, -decay * step, 0.0)
        hi = rate.astype(BF16).astype(F32)
        mid = (rate - hi).astype(BF16).astype(F32)
        low = (rate - hi - mid).astype(BF16).astype(F32)
        three = (hi + pltpu.roll(mid, HEADS, 1) + pltpu.roll(low, 2 * HEADS, 1)).astype(BF16)
        wide_t = lax.broadcasted_iota(jnp.int32, (SPAN, SPAN), 0)
        wide_s = lax.broadcasted_iota(jnp.int32, (SPAN, SPAN), 1)
        lower = jnp.where(wide_s <= wide_t, 1.0, 0.0).astype(BF16)
        sums = jnp.dot(lower, three, preferred_element_type=F32)
        logd = sums + pltpu.roll(sums, 128 - HEADS, 1) + pltpu.roll(sums, 128 - 2 * HEADS, 1)
        logd = jnp.where(lane < HEADS, logd, 0.0)
        turned = jnp.transpose(jnp.where(lane < HEADS, logd, pltpu.roll(step, HEADS, 1)))
        dots = lax.dot_general(query, keys, (((1,), (1,)), ((), ())), preferred_element_type=F32)
        wide_first = first_of(start + wide_t)
        gram[...] = jnp.where(
            (wide_s <= wide_t) & (start + wide_s >= wide_first), dots, 0.0
        )
        first_end = first_of(start + SPAN - 1)
        keep = place >= first_end
        entered = first < start
        carried = jnp.where(first_end < start, 1.0, 0.0)
        end = logd[SPAN - 1 : SPAN, :]
        re_out[j] = jnp.where(first < base, jnp.exp(logd + before), 0.0)
        across = jnp.dot(query, carry[...].astype(BF16), preferred_element_type=F32)
        c_out[j] = query
        half = SPAN // 2
        left = lane < HEAD_DIM
        left1 = lane1 < HEAD_DIM
        decays = []
        for pair in range(HEADS // 2):
            cols = slice(pair * 128, pair * 128 + 128)
            xs = conv[:, cols]
            tops, bottoms = [], []
            for h in (2 * pair, 2 * pair + 1):
                column = logd[:, h : h + 1]
                across_row = turned[h : h + 1, :]
                weight = turned[HEADS + h : HEADS + h + 1, :]
                top = jnp.exp(jnp.minimum(column[:half] - across_row[:, :half], 0.0)) * (
                    gram[:half, :half] * weight[:, :half]
                )
                bottom = jnp.exp(jnp.minimum(column[half:] - across_row, 0.0)) * (
                    gram[half:, :] * weight
                )
                tops.append(jnp.dot(top.astype(BF16), xs[:half], preferred_element_type=F32))
                bottoms.append(jnp.dot(bottom.astype(BF16), xs, preferred_element_type=F32))
            within = jnp.concatenate(
                [
                    jnp.where(left[:half], tops[0], tops[1]),
                    jnp.where(left[half:], bottoms[0], bottoms[1]),
                ],
                axis=0,
            )
            h = 2 * pair
            log2 = jnp.where(left, logd[:, h : h + 1], logd[:, h + 1 : h + 2])
            step2 = jnp.where(left, step[:, h : h + 1], step[:, h + 1 : h + 2])
            end2 = jnp.where(left1, end[:, h : h + 1], end[:, h + 1 : h + 2])
            xf = xs.astype(F32)
            inputs = jnp.where(keep, jnp.exp(end2 - log2) * step2, 0.0) * xf
            weighted[:, cols] = inputs.astype(BF16)
            reach = jnp.where(entered, jnp.exp(log2), 0.0)
            y_out[j, :, cols] = within + reach * across[:, cols] + skip_ref[:, cols] * xf
            decays.append(jnp.exp(end2) * carried)
        states = lax.dot_general(
            keys, weighted[...], (((0,), (0,)), ((), ())), preferred_element_type=F32
        )
        carry[...] = jnp.concatenate(decays, axis=1) * carry[...] + states
        return before + end

    total = lax.fori_loop(0, NX, turn, jnp.zeros((1, 128), F32))
    last = first_of(base + NX * SPAN - 1)
    lane1 = lax.broadcasted_iota(jnp.int32, (1, 128), 1)
    whole = jnp.where(last < base, jnp.exp(total), 0.0)
    spread = jnp.concatenate(
        [
            jnp.where(lane1 < HEAD_DIM, whole[:, h : h + 1], whole[:, h + 1 : h + 2])
            for h in range(0, HEADS, 2)
        ],
        axis=1,
    )
    hi = spread.astype(BF16).astype(F32)
    low = spread - hi
    which = lax.broadcasted_iota(jnp.int32, (16, WIDTH), 0)
    marks = jnp.where(which == 0, hi, jnp.where(which == 1, low, 0.0)).astype(BF16)
    parts = t_out.shape[0]
    rows = STATE // parts
    for k in range(parts):
        t_out[k, :rows] = carry[k * rows : (k + 1) * rows].astype(BF16)
        t_out[k, rows:] = marks


def scan_kernel(sc, t_ref, e_out):
    parts, rows, _ = e_out.shape
    state = jnp.zeros(e_out.shape[1:], F32)
    for k in range(parts):
        e_out[k] = state.astype(BF16)
        if k < parts - 1:
            marks = t_ref[k, rows:].astype(F32)
            state = (marks[0:1] + marks[1:2]) * state + t_ref[k, :rows].astype(F32)


def gate_kernel(sc, own, prev, nxt, far, y_ref, c_ref, re_ref, e_ref, gain_ref, v0, v1, v2, v3, sq, gate):
    x = sc[0]
    gate[x] = own[...]
    gate[around(x, 3)] = prev[...]
    gate[around(x, 1)] = nxt[...]
    gate[around(x, 2)] = far[...]
    gain = gain_ref[...]
    left = lax.broadcasted_iota(jnp.int32, (SPAN, 128), 1) < HEAD_DIM
    for j, out in enumerate((v0, v1, v2, v3)):
        across = jnp.dot(c_ref[j], e_ref[...], preferred_element_type=F32)
        reach = re_ref[j]
        total = jnp.zeros((SPAN, 128), F32)
        for pair in range(HEADS // 2):
            cols = slice(pair * 128, pair * 128 + 128)
            h = 2 * pair
            reach2 = jnp.where(left, reach[:, h : h + 1], reach[:, h + 1 : h + 2])
            g = gate[j, :, cols].astype(F32)
            v = (y_ref[j, :, cols] + reach2 * across[:, cols]) * (g * sigmoid(g))
            total = total + v * v
            out[:, cols] = (v * gain[:, cols]).astype(BF16)
        summed = jnp.broadcast_to(jnp.sum(total, axis=1, keepdims=True), (SPAN, 128))
        sq[:, j * SPAN : (j + 1) * SPAN] = jnp.transpose(summed)[:8]


def product_kernel(chunk, sc, *refs):
    blocks = (refs[0:4], refs[4:8])
    squares = refs[8:12]
    w_ref = refs[12]
    send, kept = refs[13:15]
    x, c = sc[0], sc[3]
    order = (x, around(x, 3), around(x, 1), around(x, 2))
    total = squares[0][...] + squares[1][...] + squares[2][...] + squares[3][...]
    for b in range(2):
        at = (2 * chunk + b) * SPAN
        row = jnp.broadcast_to(total[0:1, at : at + SPAN], (128, SPAN))
        mean = jnp.transpose(row) * (1.0 / (NX * WIDTH))
        scale = lax.rsqrt(mean + 1e-05)
        scale = jnp.concatenate([scale, scale], axis=1)
        for core, out in ((1 - c, send), (c, kept)):
            for yy in range(0, NY, 2):
                acc = jnp.zeros((SPAN, 256), F32)
                for part, q in zip(blocks[b], order):
                    rows = pl.ds(pl.multiple_of(q * WIDTH, WIDTH), WIDTH)
                    w = jnp.concatenate(
                        [w_ref[2 * yy + core, rows, :], w_ref[2 * yy + 2 + core, rows, :]], axis=1
                    )
                    acc = acc + jnp.dot(part[...], w, preferred_element_type=F32)
                acc = (acc * scale).astype(out.dtype)
                out[yy, b * SPAN : (b + 1) * SPAN, :] = acc[:, :128]
                out[yy + 1, b * SPAN : (b + 1) * SPAN, :] = acc[:, 128:]


def cores_kernel(sc, kept, got, to_next, to_prev, to_far, mine):
    y = sc[2]
    for by, out in ((1, to_next), (3, to_prev), (2, to_far), (0, mine)):
        q = around(y, by)
        out[...] = (kept[q] + got[q].astype(F32)).astype(out.dtype)


def rows_kernel(sc, a0, a1, a2, a3, b0, b1, b2, b3, own, to_next, to_prev, to_far, whole):
    x = sc[0]
    first = a0[...] + a1[...].astype(F32) + a2[...].astype(F32) + a3[...].astype(F32)
    second = b0[...] + b1[...].astype(F32) + b2[...].astype(F32) + b3[...].astype(F32)
    whole[0] = first[:SPAN]
    whole[1] = first[SPAN:]
    whole[2] = second[:SPAN]
    whole[3] = second[SPAN:]
    for by, out in ((0, own), (1, to_next), (3, to_prev), (2, to_far)):
        out[...] = whole[around(x, by)].astype(BF16)


def place_kernel(sc, own, prev, nxt, far, out):
    x = sc[0]
    for by, got in ((0, own), (3, prev), (1, nxt), (2, far)):
        out[:, lanes(around(x, by), 128)] = got[...]


def on_device(
    x_in, bc_in, gate_in, dt_raw, decay_rate, skip_gain, conv_x, conv_bc, norm_gain, out_weight, lengths
):
    xi, zi = lax.axis_index("x"), lax.axis_index("z")
    nz = lax.axis_size("z")
    ends = jnp.cumsum(lengths)
    sc = jnp.stack(
        [xi, zi, lax.axis_index("y"), lax.axis_index("c"), ends[0], ends[1], ends[2], ends[2]]
    ).astype(jnp.int32)
    bc = bc_in.reshape(SPAN, BC)
    w_all = lax.all_gather(out_weight, "z", axis=0)

    piece = ((SPAN, PAY), BF16)
    edge = ((16, WIDTH + BC), BF16)
    own, to_next, to_prev, to_far, *edges = call(
        pack_kernel, sc, (x_in, bc, dt_raw), [piece] * 4 + [edge] * 4,
        [pltpu.VMEM((SPAN, 128), F32)], nbytes=6 << 20,
    )
    prev, nxt, far = shift(to_next, "x", 1), shift(to_prev, "x", -1), shift(to_far, "x", 2)
    halo = [
        lax.ppermute(e, ("z", "x"), [((z - 1) * NX + NX - 1, z * NX + k) for z in range(1, nz)])
        for k, e in enumerate(edges)
    ]
    quarter = ((SPAN, WIDTH), BF16)
    g_own, g_next, g_prev, g_far = call(
        split_kernel, sc, (gate_in,), [quarter] * 4, nbytes=2 << 20
    )
    gates = (g_own, shift(g_next, "x", 1), shift(g_prev, "x", -1), shift(g_far, "x", 2))

    skip = jnp.repeat(lax.dynamic_slice(skip_gain, (xi * HEADS,), (HEADS,)), HEAD_DIM)[None, :]
    decay = jnp.pad(lax.dynamic_slice(decay_rate, (xi * HEADS,), (HEADS,)), (0, 128 - HEADS))[None, :]
    gain = lax.dynamic_slice(norm_gain, (xi * WIDTH,), (WIDTH,))[None, :]
    rows = STATE // nz
    y_loc, query, reach, sums = call(
        block_kernel, sc,
        (own, prev, nxt, far, *halo, conv_x, conv_bc.reshape(4, BC), skip, decay),
        [
            ((NX, SPAN, WIDTH), F32),
            ((NX, SPAN, STATE), BF16),
            ((NX, SPAN, 128), F32),
            ((nz, rows + 16, WIDTH), BF16),
        ],
        [
            pltpu.VMEM((NX, SPAN, PAY), BF16),
            pltpu.VMEM((SPAN + 8, WIDTH + BC), F32),
            pltpu.VMEM((SPAN, WIDTH + BC), BF16),
            pltpu.VMEM((SPAN, SPAN), F32),
            pltpu.VMEM((STATE, WIDTH), F32),
            pltpu.VMEM((SPAN, WIDTH), BF16),
        ],
        flops=4 << 30, nbytes=8 << 20,
    )
    spread = lax.all_to_all(sums, "z", 0, 0, tiled=True)
    (enter,) = call(scan_kernel, sc, (spread,), [((nz, rows, WIDTH), BF16)], nbytes=1 << 20)
    enter = lax.all_to_all(enter, "z", 0, 0, tiled=True).reshape(STATE, WIDTH)
    *v, sq = call(
        gate_kernel, sc, (*gates, y_loc, query, reach, enter, gain),
        [quarter] * 4 + [((8, NX * SPAN), F32)],
        [pltpu.VMEM((NX, SPAN, WIDTH), BF16)],
        flops=2 << 30, nbytes=6 << 20,
    )
    squares = (sq, shift(sq, "x", 1), shift(sq, "x", -1), shift(sq, "x", 2))
    parts = []
    for j, own_v in enumerate(v):
        a, b = shift(own_v, "x", 1), shift(own_v, "x", -1)
        parts.append((own_v, a, b, shift(a, "x", 1) if j % 2 == 0 else shift(b, "x", -1)))

    halves = []
    for chunk in range(2):
        send, kept = call(
            functools.partial(product_kernel, chunk), sc,
            (*parts[2 * chunk], *parts[2 * chunk + 1], *squares, w_all),
            [((NY, 2 * SPAN, 128), BF16), ((NY, 2 * SPAN, 128), F32)],
            flops=4 << 30, nbytes=8 << 20,
        )
        got = shift(send, "c", 1)
        part = ((2 * SPAN, 128), BF16)
        y_next, y_prev, y_far, mine = call(
            cores_kernel, sc, (kept, got), [part] * 3 + [((2 * SPAN, 128), F32)], nbytes=2 << 20
        )
        halves += [mine, shift(y_next, "y", 1), shift(y_prev, "y", -1), shift(y_far, "y", 2)]
    tile = ((SPAN, 128), BF16)
    own, to_next, to_prev, to_far = call(
        rows_kernel, sc, halves, [tile] * 4, [pltpu.VMEM((NX, SPAN, 128), F32)], nbytes=2 << 20
    )
    (mixed,) = call(
        place_kernel, sc,
        (own, shift(to_next, "x", 1), shift(to_prev, "x", -1), shift(to_far, "x", 2)),
        [((SPAN, NX * 128), BF16)], nbytes=1 << 20,
    )
    return mixed


def solution(mesh):
    seq, tp = ("z", "x"), ("y", "c")
    fine = Mesh(mesh.devices.reshape(mesh.devices.shape[0] // NX, NX, NY, 2), seq + tp)
    in_specs = (
        P(seq, tp),
        P(seq, tp, None),
        P(seq, tp),
        P(seq, tp),
        P(tp),
        P(tp),
        P(None, tp),
        P(None, tp, None),
        P(tp),
        P(tp, seq),
        P(),
    )
    return jax.shard_map(
        on_device, mesh=fine, in_specs=in_specs, out_specs=P(seq, tp), check_vma=False
    )
```

```python
import jax
import jax.numpy as jnp
from jax import lax
from jax.experimental import pallas as pl
from jax.experimental.pallas import tpu as pltpu
from jax.sharding import Mesh, PartitionSpec as P

SPAN = 256
NX = 4
NY = 4
HEADS = 8
HEAD_DIM = 64
WIDTH = HEADS * HEAD_DIM
STATE = 256
BC = 2 * STATE
WIDE = WIDTH + BC
F32 = jnp.float32
BF16 = jnp.bfloat16
LARGE = 48 * 1024 * 1024
SMALL = 20 * 1024 * 1024
SPECS = {
    "v": pl.BlockSpec(memory_space=pltpu.VMEM),
    "s": pl.BlockSpec(memory_space=pltpu.SMEM),
    "a": pl.BlockSpec(memory_space=pl.ANY),
    "h": pl.BlockSpec(memory_space=pl.ANY),
}


def call(kernel, spaces, args, outs, scratch=(), flops=0, nbytes=0, places=None, vmem=LARGE):
    return pl.pallas_call(
        kernel,
        in_specs=[SPECS[s] for s in spaces],
        out_specs=tuple(SPECS[s] for s in places or "v" * len(outs)),
        out_shape=tuple(jax.ShapeDtypeStruct(s, d) for s, d in outs),
        scratch_shapes=list(scratch),
        compiler_params=pltpu.CompilerParams(vmem_limit_bytes=vmem),
        cost_estimate=pl.CostEstimate(flops=flops, bytes_accessed=nbytes, transcendentals=0),
    )(*args)


def shift(v, axis, by):
    n = lax.axis_size(axis)
    return lax.ppermute(v, axis, [(i, (i + by) % n) for i in range(n)])


def around(v, by):
    return lax.rem(v + by, 4)


def sigmoid(v):
    return 0.5 * jnp.tanh(0.5 * v) + 0.5


def lanes(q, width):
    return pl.ds(pl.multiple_of(q * width, width), width)


def three_parts(v):
    hi = v.astype(BF16).astype(F32)
    mid = (v - hi).astype(BF16).astype(F32)
    return hi, mid, (v - hi - mid).astype(BF16).astype(F32)


def first_finder(lengths):
    s1 = lengths[0]
    s2 = s1 + lengths[1]
    s3 = s2 + lengths[2]
    return lambda t: jnp.where(t >= s3, s3, jnp.where(t >= s2, s2, jnp.where(t >= s1, s1, 0)))


def pack_kernel(x_any, bc_any, dt_any, own, to_next, to_prev, to_far, h0, h1, h2, h3, turned, sems):
    x = lax.axis_index("x")
    get_dt = pltpu.make_async_copy(dt_any, turned, sems.at[0])
    get_dt.start()
    copies = []

    def start(src, dst):
        copy = pltpu.make_async_copy(src, dst, sems.at[len(copies) + 1])
        copy.start()
        copies.append(copy)

    outs = ((1, to_next), (3, to_prev), (2, to_far), (0, own))
    for by, out in outs:
        q = around(x, by)
        start(x_any.at[:, lanes(q, WIDTH)], out.at[:SPAN, :WIDTH])
        start(bc_any, out.at[:SPAN, WIDTH:])
    for q, out in enumerate((h0, h1, h2, h3)):
        start(x_any.at[SPAN - 16 :, q * WIDTH : (q + 1) * WIDTH], out.at[:, :WIDTH])
        start(bc_any.at[SPAN - 16 :, :], out.at[:, WIDTH:])
    get_dt.wait()
    for by, out in outs:
        q = around(x, by)
        rows = turned[pl.ds(pl.multiple_of(q * HEADS, HEADS), HEADS), :]
        hi, mid, low = three_parts(rows)
        line = jnp.concatenate([hi, mid, low, jnp.zeros_like(low)], axis=1)
        out[SPAN:, :] = jnp.concatenate([line, jnp.zeros_like(line)], axis=0).astype(BF16)
    for copy in copies:
        copy.wait()


def split_kernel(g_any, after, own, to_next, to_prev, to_far, sems):
    x = lax.axis_index("x")
    copies = []
    for k, (by, out) in enumerate(((0, own), (1, to_next), (3, to_prev), (2, to_far))):
        copies.append(pltpu.make_async_copy(g_any.at[:, lanes(around(x, by), WIDTH)], out, sems.at[k]))
        copies[-1].start()
    for copy in copies:
        copy.wait()


def state_kernel(
    lengths, decay, own, prev, nxt, far, h0, h1, h2, h3, cw_ref, cb_ref,
    conv_hbm, cols_hbm, rows_hbm, carry_hbm, re_hbm, t_out,
    pay, ext, carry, weighted, conv_out, cols_out, rows_out, carry_out, re_out, sems,
):
    def outgoing(j):
        pairs = (
            (conv_out, conv_hbm),
            (cols_out, cols_hbm),
            (rows_out, rows_hbm),
            (carry_out, carry_hbm),
            (re_out, re_hbm),
        )
        return [
            pltpu.make_async_copy(src.at[j], dst.at[j], sems.at[k, j])
            for k, (src, dst) in enumerate(pairs)
        ]

    x = lax.axis_index("x")
    base = lax.axis_index("z") * (NX * SPAN)
    first_of = first_finder(lengths)
    pay[x] = own[...]
    pay[around(x, 3)] = prev[...]
    pay[around(x, 1)] = nxt[...]
    pay[around(x, 2)] = far[...]
    ext[0:8] = (
        h0[8:16].astype(F32) + h1[8:16].astype(F32) + h2[8:16].astype(F32) + h3[8:16].astype(F32)
    )
    carry[...] = jnp.zeros_like(carry)
    taps_x = cw_ref[:, lanes(x, WIDTH)]
    head = lax.broadcasted_iota(jnp.int32, (HEADS, SPAN), 0)
    rates = jnp.zeros((HEADS, SPAN), F32)
    for h in range(HEADS):
        rates = jnp.where(head == h, decay[x * HEADS + h], rates)

    def turn(j, before):
        start = base + j * SPAN

        @pl.when(j > 0)
        def _():
            ext[0:8] = ext[SPAN : SPAN + 8]

        ext[8:] = pay[j, :SPAN, :].astype(F32)
        row = lax.broadcasted_iota(jnp.int32, (SPAN, 128), 0)
        lane = lax.broadcasted_iota(jnp.int32, (SPAN, 128), 1)
        lane1 = lax.broadcasted_iota(jnp.int32, (1, 128), 1)
        place = start + row
        first = first_of(place)
        pos = place - first
        for part in range(WIDE // 128):
            at = part * 128
            cols = slice(at, at + 128)

            def tap(k):
                if at < WIDTH:
                    return taps_x[k : k + 1, cols]
                return cb_ref[k][:, at - WIDTH : at - WIDTH + 128]

            acc = tap(3) * ext[8 : 8 + SPAN, cols]
            for back in (1, 2, 3):
                term = tap(3 - back) * ext[8 - back : 8 - back + SPAN, cols]
                acc = acc + jnp.where(pos >= back, term, 0.0)
            conv_out[j, :, cols] = (acc * sigmoid(acc)).astype(BF16)
        packed = pay[j, SPAN:, :][:HEADS].astype(F32)
        raw = packed[:, :SPAN] + packed[:, SPAN : 2 * SPAN] + packed[:, 2 * SPAN : 3 * SPAN]
        step = jnp.maximum(raw, 0.0) + jnp.log1p(jnp.exp(-jnp.abs(raw)))
        parts = jnp.concatenate(
            [*three_parts(-rates * step), jnp.zeros((HEADS, SPAN), F32)], axis=0
        ).astype(BF16)
        wide_s = lax.broadcasted_iota(jnp.int32, (SPAN, SPAN), 0)
        wide_t = lax.broadcasted_iota(jnp.int32, (SPAN, SPAN), 1)
        upper = jnp.where(wide_s <= wide_t, 1.0, 0.0).astype(BF16)
        sums = jnp.dot(parts, upper, preferred_element_type=F32)
        logd = sums[:HEADS] + sums[HEADS : 2 * HEADS] + sums[2 * HEADS : 3 * HEADS]
        both = jnp.concatenate([logd, step], axis=0)
        rows_out[j] = both
        cols = jnp.transpose(
            jnp.concatenate([both, jnp.zeros((128 - 2 * HEADS, SPAN), F32)], axis=0)
        )
        cols_out[j] = cols
        first_end = first_of(start + SPAN - 1)
        keep = place >= first_end
        carried = jnp.where(first_end < start, 1.0, 0.0)
        end = cols[SPAN - 1 : SPAN, :]
        re_out[j] = jnp.where(first < base, jnp.exp(jnp.minimum(cols + before, 0.0)), 0.0)
        left = lane < HEAD_DIM
        left1 = lane1 < HEAD_DIM
        decays = []
        for pair in range(HEADS // 2):
            at = slice(pair * 128, pair * 128 + 128)
            h = 2 * pair
            log2 = jnp.where(left, cols[:, h : h + 1], cols[:, h + 1 : h + 2])
            s = HEADS + h
            step2 = jnp.where(left, cols[:, s : s + 1], cols[:, s + 1 : s + 2])
            end2 = jnp.where(left1, end[:, h : h + 1], end[:, h + 1 : h + 2])
            inputs = jnp.where(keep, jnp.exp(end2 - log2) * step2, 0.0) * conv_out[j, :, at].astype(F32)
            weighted[:, at] = inputs.astype(BF16)
            decays.append(jnp.exp(end2) * carried)
        keys = conv_out[j, :, WIDTH : WIDTH + STATE]
        states = lax.dot_general(
            keys, weighted[...], (((0,), (0,)), ((), ())), preferred_element_type=F32
        )
        state = carry[...]
        carry_out[j] = state.astype(BF16)
        carry[...] = jnp.concatenate(decays, axis=1) * state + states
        for copy in outgoing(j):
            copy.start()
        return before + jnp.where(lane1 < HEADS, end, 0.0)

    total = lax.fori_loop(0, NX, turn, jnp.zeros((1, 128), F32))
    last = first_of(base + NX * SPAN - 1)
    lane1 = lax.broadcasted_iota(jnp.int32, (1, 128), 1)
    whole = jnp.where(last < base, jnp.exp(total), 0.0)
    spread = jnp.concatenate(
        [
            jnp.where(lane1 < HEAD_DIM, whole[:, h : h + 1], whole[:, h + 1 : h + 2])
            for h in range(0, HEADS, 2)
        ],
        axis=1,
    )
    hi = spread.astype(BF16).astype(F32)
    which = lax.broadcasted_iota(jnp.int32, (16, WIDTH), 0)
    marks = jnp.where(which == 0, hi, jnp.where(which == 1, spread - hi, 0.0)).astype(BF16)
    parts = t_out.shape[0]
    rows = STATE // parts
    for k in range(parts):
        t_out[k, :rows] = carry[k * rows : (k + 1) * rows].astype(BF16)
        t_out[k, rows:] = marks

    def finish(j, token):
        for copy in outgoing(j):
            copy.wait()
        return token

    lax.fori_loop(0, NX, finish, 0)


def within_kernel(
    lengths, skip, conv_hbm, cols_hbm, rows_hbm, carry_hbm, after, y_hbm,
    gram, conv_ref, cols_ref, rows_ref, carry_ref, y_out, sems,
):
    def incoming(j):
        pairs = (
            (conv_hbm, conv_ref),
            (cols_hbm, cols_ref),
            (rows_hbm, rows_ref),
            (carry_hbm, carry_ref),
        )
        return [
            pltpu.make_async_copy(src.at[j], dst.at[j], sems.at[k, j])
            for k, (src, dst) in enumerate(pairs)
        ]

    def result(j):
        return pltpu.make_async_copy(y_out.at[j], y_hbm.at[j], sems.at[4, j])

    def begin(j, token):
        for copy in incoming(j):
            copy.start()
        return token

    lax.fori_loop(0, NX, begin, 0)
    x = lax.axis_index("x")
    base = lax.axis_index("z") * (NX * SPAN)
    first_of = first_finder(lengths)
    half = SPAN // 2

    def turn(j, token):
        for copy in incoming(j):
            copy.wait()
        start = base + j * SPAN
        row = lax.broadcasted_iota(jnp.int32, (SPAN, 128), 0)
        lane = lax.broadcasted_iota(jnp.int32, (SPAN, 128), 1)
        left = lane < HEAD_DIM
        left1 = lax.broadcasted_iota(jnp.int32, (1, 128), 1) < HEAD_DIM
        entered = first_of(start + row) < start
        keys = conv_ref[j, :, WIDTH : WIDTH + STATE]
        query = conv_ref[j, :, WIDTH + STATE :]
        dots = lax.dot_general(query, keys, (((1,), (1,)), ((), ())), preferred_element_type=F32)
        wide_t = lax.broadcasted_iota(jnp.int32, (SPAN, SPAN), 0)
        wide_s = lax.broadcasted_iota(jnp.int32, (SPAN, SPAN), 1)
        wide_first = first_of(start + wide_t)
        gram[...] = jnp.where((wide_s <= wide_t) & (start + wide_s >= wide_first), dots, 0.0)
        across = jnp.dot(query, carry_ref[j], preferred_element_type=F32)
        cols = cols_ref[j]
        rows = rows_ref[j]
        for pair in range(HEADS // 2):
            at = slice(pair * 128, pair * 128 + 128)
            xs = conv_ref[j, :, at]
            tops, bottoms = [], []
            for h in (2 * pair, 2 * pair + 1):
                column = cols[:, h : h + 1]
                log_row = rows[h : h + 1, :]
                weight = rows[HEADS + h : HEADS + h + 1, :]
                top = jnp.exp(jnp.minimum(column[:half] - log_row[:, :half], 0.0)) * (
                    gram[:half, :half] * weight[:, :half]
                )
                bottom = jnp.exp(jnp.minimum(column[half:] - log_row, 0.0)) * (
                    gram[half:, :] * weight
                )
                tops.append(jnp.dot(top.astype(BF16), xs[:half], preferred_element_type=F32))
                bottoms.append(jnp.dot(bottom.astype(BF16), xs, preferred_element_type=F32))
            within = jnp.concatenate(
                [
                    jnp.where(left[:half], tops[0], tops[1]),
                    jnp.where(left[half:], bottoms[0], bottoms[1]),
                ],
                axis=0,
            )
            h = 2 * pair
            log2 = jnp.where(left, cols[:, h : h + 1], cols[:, h + 1 : h + 2])
            reach = jnp.where(entered, jnp.exp(log2), 0.0)
            direct = jnp.where(left1, skip[x * HEADS + h], skip[x * HEADS + h + 1])
            y_out[j, :, at] = within + reach * across[:, at] + direct * xs.astype(F32)
        result(j).start()
        return token

    lax.fori_loop(0, NX, turn, 0)

    def finish(j, token):
        result(j).wait()
        return token

    lax.fori_loop(0, NX, finish, 0)


def scan_kernel(t_ref, *refs):
    e_out = refs[-1]
    parts, rows, _ = e_out.shape
    state = jnp.zeros(e_out.shape[1:], F32)
    for k in range(parts):
        e_out[k] = state.astype(BF16)
        if k < parts - 1:
            marks = t_ref[k, rows:].astype(F32)
            state = (marks[0:1] + marks[1:2]) * state + t_ref[k, :rows].astype(F32)


def gate_kernel(own, prev, nxt, far, y_hbm, conv_hbm, re_hbm, e_ref, gain_ref, *refs):
    *outs, gate, y_ref, query, re_ref, sems = refs[1:]
    x = lax.axis_index("x")
    copies = []
    for j in range(NX):
        b = j
        for src, dst in (
            (y_hbm.at[j], y_ref.at[b]),
            (conv_hbm.at[j, :, WIDTH + STATE :], query.at[b]),
            (re_hbm.at[j], re_ref.at[b]),
        ):
            copies.append(pltpu.make_async_copy(src, dst, sems.at[len(copies)]))
            copies[-1].start()
    gets = []
    for k, (by, src) in enumerate(((0, own), (3, prev), (1, nxt), (2, far))):
        gets.append(pltpu.make_async_copy(src, gate.at[around(x, by)], sems.at[12 + k]))
        gets[-1].start()
    for get in gets:
        get.wait()
    gain = gain_ref[:, lanes(x, WIDTH)]
    left = lax.broadcasted_iota(jnp.int32, (SPAN, 128), 1) < HEAD_DIM
    for b, out in enumerate(outs):
        for copy in copies[3 * b : 3 * b + 3]:
            copy.wait()
        across = jnp.dot(query[b], e_ref[...], preferred_element_type=F32)
        reach = re_ref[b]
        for pair in range(HEADS // 2):
            cols = slice(pair * 128, pair * 128 + 128)
            h = 2 * pair
            reach2 = jnp.where(left, reach[:, h : h + 1], reach[:, h + 1 : h + 2])
            g = gate[b, :, cols].astype(F32)
            v = (y_ref[b, :, cols] + reach2 * across[:, cols]) * (g * sigmoid(g))
            out[:, cols] = (v * gain[:, cols]).astype(BF16)


def product_kernel(*refs):
    gain_ref, w_ref = refs[8:10]
    send, kept, left = refs[-3:]
    x, c = lax.axis_index("x"), lax.axis_index("c")
    order = (x, around(x, 3), around(x, 1), around(x, 2))
    for k, ref in enumerate(refs[:8]):
        left[k // 4 * SPAN : k // 4 * SPAN + SPAN, lanes(order[k % 4], WIDTH)] = ref[...]
    plain = left[...] * (1.0 / gain_ref[...]).astype(BF16)
    ones = jnp.ones((NX * WIDTH, 128), BF16)
    mean = jnp.dot(plain * plain, ones, preferred_element_type=F32) * (1.0 / (NX * WIDTH))
    scale = lax.rsqrt(mean + 1e-05)
    scale = jnp.concatenate([scale, scale], axis=1)
    for core, out in ((1 - c, send), (c, kept)):
        for yy in range(0, NY, 2):
            w = jnp.concatenate([w_ref[2 * yy + core], w_ref[2 * yy + 2 + core]], axis=1)
            acc = jnp.dot(left[...], w, preferred_element_type=F32)
            acc = (acc * scale).astype(out.dtype)
            out[yy] = acc[:, :128]
            out[yy + 1] = acc[:, 128:]


def hold_kernel(w_any, after, out, sem):
    copy = pltpu.make_async_copy(w_any, out, sem)
    copy.start()
    copy.wait()


def cores_kernel(kept, got, to_next, to_prev, to_far, mine):
    y = lax.axis_index("y")
    for by, out in ((1, to_next), (3, to_prev), (2, to_far), (0, mine)):
        q = around(y, by)
        out[...] = (kept[q] + got[q].astype(F32)).astype(out.dtype)


def rows_kernel(a0, a1, a2, a3, b0, b1, b2, b3, own, to_next, to_prev, to_far, whole):
    x = lax.axis_index("x")
    first = a0[...] + a1[...].astype(F32) + a2[...].astype(F32) + a3[...].astype(F32)
    second = b0[...] + b1[...].astype(F32) + b2[...].astype(F32) + b3[...].astype(F32)
    whole[0] = first[:SPAN]
    whole[1] = first[SPAN:]
    whole[2] = second[:SPAN]
    whole[3] = second[SPAN:]
    for by, out in ((0, own), (1, to_next), (3, to_prev), (2, to_far)):
        out[...] = whole[around(x, by)].astype(BF16)


def place_kernel(own, prev, nxt, far, out):
    x = lax.axis_index("x")
    for by, got in ((0, own), (3, prev), (1, nxt), (2, far)):
        out[:, lanes(around(x, by), 128)] = got[...]


def on_device(
    x_in, bc_in, gate_in, dt_raw, decay_rate, skip_gain, conv_x, conv_bc, norm_gain, out_weight, lengths
):
    nz = lax.axis_size("z")
    bc = bc_in.reshape(SPAN, BC)
    w_all = lax.all_gather(out_weight, "z", axis=0)

    piece = ((SPAN + 16, WIDE), BF16)
    edge = ((16, WIDE), BF16)
    own, to_next, to_prev, to_far, *edges = call(
        pack_kernel, "hhh", (x_in, bc, dt_raw.T), [piece] * 4 + [edge] * 4,
        [
            pltpu.VMEM((4 * HEADS, SPAN), F32),
            pltpu.SemaphoreType.DMA((17,)),
        ],
        nbytes=6 << 20,
    )
    far = shift(to_far, "x", 2)
    prev, nxt = shift(to_next, "x", 1), shift(to_prev, "x", -1)
    halo = [
        lax.ppermute(e, ("z", "x"), [((z - 1) * NX + NX - 1, z * NX + k) for z in range(1, nz)])
        for k, e in enumerate(edges)
    ]
    quarter = ((SPAN, WIDTH), BF16)
    g_own, g_next, g_prev, g_far = call(
        split_kernel, "ha", (gate_in, far), [quarter] * 4, [pltpu.SemaphoreType.DMA((4,))],
        nbytes=2 << 20,
    )
    gates = (g_own, shift(g_next, "x", 1), shift(g_prev, "x", -1), shift(g_far, "x", 2))

    gain = norm_gain[None, :]
    rows = STATE // nz
    kept_specs = [
        pltpu.VMEM((NX, SPAN, WIDE), BF16),
        pltpu.VMEM((NX, SPAN, 128), F32),
        pltpu.VMEM((NX, 2 * HEADS, SPAN), F32),
        pltpu.VMEM((NX, STATE, WIDTH), BF16),
        pltpu.VMEM((NX, SPAN, 128), F32),
    ]
    conv, cols, lines, carry, reach, sums = call(
        state_kernel, "ss" + "v" * 10,
        (lengths, decay_rate, own, prev, nxt, far, *halo, conv_x, conv_bc),
        [
            ((NX, SPAN, WIDE), BF16),
            ((NX, SPAN, 128), F32),
            ((NX, 2 * HEADS, SPAN), F32),
            ((NX, STATE, WIDTH), BF16),
            ((NX, SPAN, 128), F32),
            ((nz, rows + 16, WIDTH), BF16),
        ],
        [
            pltpu.VMEM((NX, SPAN + 16, WIDE), BF16),
            pltpu.VMEM((SPAN + 8, WIDE), F32),
            pltpu.VMEM((STATE, WIDTH), F32),
            pltpu.VMEM((SPAN, WIDTH), BF16),
            *kept_specs,
            pltpu.SemaphoreType.DMA((5, NX)),
        ],
        flops=4 << 30, nbytes=16 << 20, places="hhhhhv",
    )
    spread = lax.all_to_all(sums, "z", 0, 0, tiled=True)
    (y_loc,) = call(
        within_kernel, "sshhhha", (lengths, skip_gain, conv, cols, lines, carry, g_own),
        [((NX, SPAN, WIDTH), F32)],
        [
            pltpu.VMEM((SPAN, SPAN), F32),
            *kept_specs[:4],
            pltpu.VMEM((NX, SPAN, WIDTH), F32),
            pltpu.SemaphoreType.DMA((5, NX)),
        ],
        flops=6 << 30, nbytes=16 << 20, places="h",
    )
    (enter,) = call(
        scan_kernel, "vhaaa", (spread, y_loc, *gates[1:]), [((nz, rows, WIDTH), BF16)], nbytes=1 << 20
    )
    enter = lax.all_to_all(enter, "z", 0, 0, tiled=True).reshape(STATE, WIDTH)

    halves = []
    v = call(
        gate_kernel, "aaaahhhvva", (*gates, y_loc, conv, reach, enter, gain, w_all),
        [quarter] * NX,
        [
            pltpu.VMEM((NX, SPAN, WIDTH), BF16),
            pltpu.VMEM((NX, SPAN, WIDTH), F32),
            pltpu.VMEM((NX, SPAN, STATE), BF16),
            pltpu.VMEM((NX, SPAN, 128), F32),
            pltpu.SemaphoreType.DMA((16,)),
        ],
        flops=2 << 30, nbytes=6 << 20,
    )
    parts = []
    for k, o in enumerate(v):
        a, b = shift(o, "x", 1), shift(o, "x", -1)
        parts += [o, a, b, shift(a, "x", 1) if k % 2 == 0 else shift(b, "x", -1)]
    gathered = (parts[:8], parts[8:])
    (w_near,) = call(
        hold_kernel, "aa", (w_all, v[-1]), [((nz, NX * WIDTH, 128), BF16)],
        [pltpu.SemaphoreType.DMA(())], nbytes=1 << 20, vmem=SMALL,
    )
    after = tuple(parts[k] for k in (9, 10, 11, 13, 14, 15))
    for parts in gathered:
        send, kept = call(
            product_kernel, "v" * 10 + "a" * len(after), (*parts, gain, w_near, *after),
            [((NY, 2 * SPAN, 128), BF16), ((NY, 2 * SPAN, 128), F32)],
            [
                pltpu.VMEM((2 * SPAN, NX * WIDTH), BF16),
            ],
            flops=3 << 30, nbytes=8 << 20, vmem=SMALL,
        )
        got = shift(send, "c", 1)
        part = ((2 * SPAN, 128), BF16)
        y_next, y_prev, y_far, mine = call(
            cores_kernel, "vv", (kept, got), [part] * 3 + [((2 * SPAN, 128), F32)], nbytes=2 << 20, vmem=SMALL
        )
        after = ()
        halves += [mine, shift(y_next, "y", 1), shift(y_prev, "y", -1), shift(y_far, "y", 2)]
    tile = ((SPAN, 128), BF16)
    own, to_next, to_prev, to_far = call(
        rows_kernel, "v" * 8, halves, [tile] * 4, [pltpu.VMEM((NX, SPAN, 128), F32)], nbytes=2 << 20, vmem=SMALL
    )
    (mixed,) = call(
        place_kernel, "vvvv",
        (own, shift(to_next, "x", 1), shift(to_prev, "x", -1), shift(to_far, "x", 2)),
        [((SPAN, NX * 128), BF16)], nbytes=1 << 20, vmem=SMALL,
    )
    return mixed


def solution(mesh):
    seq, tp = ("z", "x"), ("y", "c")
    fine = Mesh(mesh.devices.reshape(mesh.devices.shape[0] // NX, NX, NY, 2), seq + tp)
    in_specs = (
        P(seq, tp),
        P(seq, tp, None),
        P(seq, tp),
        P(seq, tp),
        P(tp),
        P(tp),
        P(None, tp),
        P(None, tp, None),
        P(tp),
        P(tp, seq),
        P(),
    )
    return jax.shard_map(
        on_device, mesh=fine, in_specs=in_specs, out_specs=P(seq, tp), check_vma=False
    )
```

```python
import jax
import jax.numpy as jnp
from jax import lax
from jax.experimental import pallas as pl
from jax.experimental.pallas import tpu as pltpu
from jax.sharding import Mesh, PartitionSpec as P

SPAN = 256
NX = 4
NY = 4
HEADS = 8
HEAD_DIM = 64
WIDTH = HEADS * HEAD_DIM
STATE = 256
BC = 2 * STATE
WIDE = WIDTH + BC
F32 = jnp.float32
BF16 = jnp.bfloat16
LARGE = 60 * 1024 * 1024
SMALL = 20 * 1024 * 1024
SPECS = {
    "v": pl.BlockSpec(memory_space=pltpu.VMEM),
    "s": pl.BlockSpec(memory_space=pltpu.SMEM),
    "a": pl.BlockSpec(memory_space=pl.ANY),
    "h": pl.BlockSpec(memory_space=pl.ANY),
}


def call(kernel, spaces, args, outs, scratch=(), flops=0, nbytes=0, places=None, vmem=LARGE):
    return pl.pallas_call(
        kernel,
        in_specs=[SPECS[s] for s in spaces],
        out_specs=tuple(SPECS[s] for s in places or "v" * len(outs)),
        out_shape=tuple(jax.ShapeDtypeStruct(s, d) for s, d in outs),
        scratch_shapes=list(scratch),
        compiler_params=pltpu.CompilerParams(vmem_limit_bytes=vmem),
        cost_estimate=pl.CostEstimate(flops=flops, bytes_accessed=nbytes, transcendentals=0),
    )(*args)


def shift(v, axis, by):
    n = lax.axis_size(axis)
    return lax.ppermute(v, axis, [(i, (i + by) % n) for i in range(n)])


def around(v, by):
    return lax.rem(v + by, 4)


def sigmoid(v):
    return 0.5 * jnp.tanh(0.5 * v) + 0.5


def lanes(q, width):
    return pl.ds(pl.multiple_of(q * width, width), width)


def three_parts(v):
    hi = v.astype(BF16).astype(F32)
    mid = (v - hi).astype(BF16).astype(F32)
    return hi, mid, (v - hi - mid).astype(BF16).astype(F32)


def first_finder(lengths):
    s1 = lengths[0]
    s2 = s1 + lengths[1]
    s3 = s2 + lengths[2]
    return lambda t: jnp.where(t >= s3, s3, jnp.where(t >= s2, s2, jnp.where(t >= s1, s1, 0)))


def pack_kernel(x_any, bc_any, dt_any, *refs):
    bcs, xs, edges = refs[0:4], refs[4:8], refs[8:12]
    turned, sems = refs[12:]
    x = lax.axis_index("x")
    get_dt = pltpu.make_async_copy(dt_any, turned, sems.at[0])
    get_dt.start()
    copies = []

    def start(src, dst):
        copy = pltpu.make_async_copy(src, dst, sems.at[len(copies) + 1])
        copy.start()
        copies.append(copy)

    order = (1, 3, 2, 0)
    for out in bcs:
        start(bc_any, out.at[:SPAN, :])
    for by, out in zip(order, xs):
        start(x_any.at[:, lanes(around(x, by), WIDTH)], out)
    for q, out in enumerate(edges):
        start(x_any.at[SPAN - 16 :, q * WIDTH : (q + 1) * WIDTH], out.at[:, :WIDTH])
        start(bc_any.at[SPAN - 16 :, :], out.at[:, WIDTH:])
    get_dt.wait()
    for by, out in zip(order, bcs):
        rows = turned[pl.ds(pl.multiple_of(around(x, by) * HEADS, HEADS), HEADS), :]
        hi, mid, low = three_parts(rows)
        upper = jnp.concatenate([hi, mid], axis=1)
        lower = jnp.concatenate([low, jnp.zeros_like(low)], axis=1)
        out[SPAN:, :] = jnp.concatenate([upper, lower], axis=0).astype(BF16)
    for copy in copies:
        copy.wait()


def split_kernel(g_any, after, own, to_next, to_prev, to_far, sems):
    x = lax.axis_index("x")
    copies = []
    for k, (by, out) in enumerate(((0, own), (1, to_next), (3, to_prev), (2, to_far))):
        copies.append(pltpu.make_async_copy(g_any.at[:, lanes(around(x, by), WIDTH)], out, sems.at[k]))
        copies[-1].start()
    for copy in copies:
        copy.wait()


def convolve(ext, tap, pos, at):
    cols = slice(at, at + 128)
    acc = tap(3, at) * ext[8 : 8 + SPAN, cols]
    for back in (1, 2, 3):
        term = tap(3 - back, at) * ext[8 - back : 8 - back + SPAN, cols]
        acc = acc + jnp.where(pos >= back, term, 0.0)
    return (acc * sigmoid(acc)).astype(BF16)


def step_kernel(
    lengths, decay, h0, h1, h2, h3, own, prev, nxt, far, cb_ref,
    bc_hbm, cols_hbm, rows_hbm, re_hbm, total_out,
    pay, ext, bc_out, cols_out, rows_out, re_out, sems,
):
    def outgoing(j):
        pairs = ((bc_out, bc_hbm), (cols_out, cols_hbm), (rows_out, rows_hbm), (re_out, re_hbm))
        return [
            pltpu.make_async_copy(src.at[j], dst.at[j], sems.at[k, j])
            for k, (src, dst) in enumerate(pairs)
        ]

    x = lax.axis_index("x")
    base = lax.axis_index("z") * (NX * SPAN)
    first_of = first_finder(lengths)
    for by, src in ((0, own), (3, prev), (1, nxt), (2, far)):
        pay[around(x, by)] = src[...]
    cut = slice(WIDTH, WIDTH + BC)
    ext[0:8] = (
        h0[8:16, cut].astype(F32)
        + h1[8:16, cut].astype(F32)
        + h2[8:16, cut].astype(F32)
        + h3[8:16, cut].astype(F32)
    )
    head = lax.broadcasted_iota(jnp.int32, (HEADS, SPAN), 0)
    rates = jnp.zeros((HEADS, SPAN), F32)
    for h in range(HEADS):
        rates = jnp.where(head == h, decay[x * HEADS + h], rates)
    raw = []
    for j in range(NX):
        packed = pay[j, SPAN:, :].astype(F32)
        raw.append(packed[:HEADS, :SPAN] + packed[:HEADS, SPAN:] + packed[HEADS:, :SPAN])
    raw = jnp.concatenate(raw, axis=0)
    step = jnp.maximum(raw, 0.0) + jnp.log1p(jnp.exp(-jnp.abs(raw)))
    rate = -jnp.concatenate([rates] * NX, axis=0) * step
    parts = jnp.concatenate([*three_parts(rate), jnp.zeros_like(rate)], axis=0).astype(BF16)
    wide_s = lax.broadcasted_iota(jnp.int32, (SPAN, SPAN), 0)
    wide_t = lax.broadcasted_iota(jnp.int32, (SPAN, SPAN), 1)
    upper = jnp.where(wide_s <= wide_t, 1.0, 0.0).astype(BF16)
    sums = jnp.dot(parts, upper, preferred_element_type=F32)
    n = NX * HEADS
    logd = sums[:n] + sums[n : 2 * n] + sums[2 * n : 3 * n]
    row = lax.broadcasted_iota(jnp.int32, (SPAN, 128), 0)
    lane1 = lax.broadcasted_iota(jnp.int32, (1, 128), 1)
    before = jnp.zeros((1, 128), F32)
    for j in range(NX):
        at = slice(j * HEADS, (j + 1) * HEADS)
        both = jnp.concatenate([logd[at], step[at]], axis=0)
        rows_out[j] = both
        cols = jnp.transpose(
            jnp.concatenate([both, jnp.zeros((128 - 2 * HEADS, SPAN), F32)], axis=0)
        )
        cols_out[j] = cols
        first = first_of(base + j * SPAN + row)
        re_out[j] = jnp.where(first < base, jnp.exp(jnp.minimum(cols + before, 0.0)), 0.0)
        before = before + jnp.where(lane1 < HEADS, cols[SPAN - 1 : SPAN, :], 0.0)
    total_out[...] = jnp.broadcast_to(before, total_out.shape)

    def turn(j, token):
        @pl.when(j > 0)
        def _():
            ext[0:8] = ext[SPAN : SPAN + 8]

        ext[8:] = pay[j, :SPAN, :].astype(F32)
        place = base + j * SPAN + row
        pos = place - first_of(place)
        for part in range(BC // 128):
            at = part * 128
            bc_out[j, :, at : at + 128] = convolve(
                ext, lambda k, at: cb_ref[k][:, at : at + 128], pos, at
            )
        for copy in outgoing(j):
            copy.start()
        return token

    lax.fori_loop(0, NX, turn, 0)

    def finish(j, token):
        for copy in outgoing(j):
            copy.wait()
        return token

    lax.fori_loop(0, NX, finish, 0)


def state_kernel(
    lengths, own, prev, nxt, far, h0, h1, h2, h3, cw_ref, bc_ref, cols_ref, total_ref,
    xs_hbm, carry_hbm, t_out,
    pay, ext, carry, weighted, xs_out, carry_out, sems,
):
    def outgoing(j):
        pairs = ((xs_out, xs_hbm), (carry_out, carry_hbm))
        return [
            pltpu.make_async_copy(src.at[j], dst.at[j], sems.at[k, j])
            for k, (src, dst) in enumerate(pairs)
        ]

    x = lax.axis_index("x")
    base = lax.axis_index("z") * (NX * SPAN)
    first_of = first_finder(lengths)
    for by, src in ((0, own), (3, prev), (1, nxt), (2, far)):
        pay[around(x, by)] = src[...]
    ext[0:8] = (
        h0[8:16, :WIDTH].astype(F32)
        + h1[8:16, :WIDTH].astype(F32)
        + h2[8:16, :WIDTH].astype(F32)
        + h3[8:16, :WIDTH].astype(F32)
    )
    carry[...] = jnp.zeros_like(carry)
    taps = cw_ref[:, lanes(x, WIDTH)]
    row = lax.broadcasted_iota(jnp.int32, (SPAN, 128), 0)
    left = lax.broadcasted_iota(jnp.int32, (SPAN, 128), 1) < HEAD_DIM
    left1 = lax.broadcasted_iota(jnp.int32, (1, 128), 1) < HEAD_DIM

    def turn(j, token):
        start = base + j * SPAN

        @pl.when(j > 0)
        def _():
            ext[0:8] = ext[SPAN : SPAN + 8]

        ext[8:] = pay[j].astype(F32)
        place = start + row
        pos = place - first_of(place)
        first_end = first_of(start + SPAN - 1)
        keep = place >= first_end
        carried = jnp.where(first_end < start, 1.0, 0.0)
        cols = cols_ref[j]
        end = cols[SPAN - 1 : SPAN, :]
        decays = []
        for pair in range(HEADS // 2):
            at = slice(pair * 128, pair * 128 + 128)
            h = 2 * pair
            xs = convolve(ext, lambda k, at: taps[k : k + 1, at : at + 128], pos, pair * 128)
            xs_out[j, :, at] = xs
            log2 = jnp.where(left, cols[:, h : h + 1], cols[:, h + 1 : h + 2])
            s = HEADS + h
            step2 = jnp.where(left, cols[:, s : s + 1], cols[:, s + 1 : s + 2])
            end2 = jnp.where(left1, end[:, h : h + 1], end[:, h + 1 : h + 2])
            inputs = jnp.where(keep, jnp.exp(end2 - log2) * step2, 0.0) * xs.astype(F32)
            weighted[:, at] = inputs.astype(BF16)
            decays.append(jnp.exp(end2) * carried)
        states = lax.dot_general(
            bc_ref[j, :, :STATE], weighted[...], (((0,), (0,)), ((), ())), preferred_element_type=F32
        )
        state = carry[...]
        carry_out[j] = state.astype(BF16)
        carry[...] = jnp.concatenate(decays, axis=1) * state + states
        for copy in outgoing(j):
            copy.start()
        return token

    lax.fori_loop(0, NX, turn, 0)
    last = first_of(base + NX * SPAN - 1)
    whole = jnp.where(last < base, jnp.exp(total_ref[0:1, :]), 0.0)
    spread = jnp.concatenate(
        [
            jnp.where(left1, whole[:, h : h + 1], whole[:, h + 1 : h + 2])
            for h in range(0, HEADS, 2)
        ],
        axis=1,
    )
    hi = spread.astype(BF16).astype(F32)
    which = lax.broadcasted_iota(jnp.int32, (16, WIDTH), 0)
    marks = jnp.where(which == 0, hi, jnp.where(which == 1, spread - hi, 0.0)).astype(BF16)
    parts = t_out.shape[0]
    rows = STATE // parts
    for k in range(parts):
        t_out[k, :rows] = carry[k * rows : (k + 1) * rows].astype(BF16)
        t_out[k, rows:] = marks

    def finish(j, token):
        for copy in outgoing(j):
            copy.wait()
        return token

    lax.fori_loop(0, NX, finish, 0)


def within_kernel(
    lengths, skip, xs_hbm, bc_hbm, cols_hbm, rows_hbm, carry_hbm, *refs
):
    y_hbm, gram, xs_ref, bc_ref, cols_ref, rows_ref, carry_ref, y_out, sems = refs[-9:]

    def incoming(j):
        pairs = (
            (xs_hbm, xs_ref),
            (bc_hbm, bc_ref),
            (cols_hbm, cols_ref),
            (rows_hbm, rows_ref),
            (carry_hbm, carry_ref),
        )
        return [
            pltpu.make_async_copy(src.at[j], dst.at[j], sems.at[k, j])
            for k, (src, dst) in enumerate(pairs)
        ]

    def result(j):
        return pltpu.make_async_copy(y_out.at[j], y_hbm.at[j], sems.at[5, j])

    def begin(j, token):
        for copy in incoming(j):
            copy.start()
        return token

    lax.fori_loop(0, NX, begin, 0)
    x = lax.axis_index("x")
    base = lax.axis_index("z") * (NX * SPAN)
    first_of = first_finder(lengths)
    half = SPAN // 2

    def turn(j, token):
        for copy in incoming(j):
            copy.wait()
        start = base + j * SPAN
        row = lax.broadcasted_iota(jnp.int32, (SPAN, 128), 0)
        lane = lax.broadcasted_iota(jnp.int32, (SPAN, 128), 1)
        left = lane < HEAD_DIM
        left1 = lax.broadcasted_iota(jnp.int32, (1, 128), 1) < HEAD_DIM
        entered = first_of(start + row) < start
        keys = bc_ref[j, :, :STATE]
        query = bc_ref[j, :, STATE:]
        dots = lax.dot_general(query, keys, (((1,), (1,)), ((), ())), preferred_element_type=F32)
        wide_t = lax.broadcasted_iota(jnp.int32, (SPAN, SPAN), 0)
        wide_s = lax.broadcasted_iota(jnp.int32, (SPAN, SPAN), 1)
        wide_first = first_of(start + wide_t)
        gram[...] = jnp.where((wide_s <= wide_t) & (start + wide_s >= wide_first), dots, 0.0)
        across = jnp.dot(query, carry_ref[j], preferred_element_type=F32)
        cols = cols_ref[j]
        rows = rows_ref[j]
        for pair in range(HEADS // 2):
            at = slice(pair * 128, pair * 128 + 128)
            xs = xs_ref[j, :, at]
            tops, bottoms = [], []
            for h in (2 * pair, 2 * pair + 1):
                column = cols[:, h : h + 1]
                log_row = rows[h : h + 1, :]
                weight = rows[HEADS + h : HEADS + h + 1, :]
                top = jnp.exp(jnp.minimum(column[:half] - log_row[:, :half], 0.0)) * (
                    gram[:half, :half] * weight[:, :half]
                )
                bottom = jnp.exp(jnp.minimum(column[half:] - log_row, 0.0)) * (
                    gram[half:, :] * weight
                )
                tops.append(jnp.dot(top.astype(BF16), xs[:half], preferred_element_type=F32))
                bottoms.append(jnp.dot(bottom.astype(BF16), xs, preferred_element_type=F32))
            within = jnp.concatenate(
                [
                    jnp.where(left[:half], tops[0], tops[1]),
                    jnp.where(left[half:], bottoms[0], bottoms[1]),
                ],
                axis=0,
            )
            h = 2 * pair
            log2 = jnp.where(left, cols[:, h : h + 1], cols[:, h + 1 : h + 2])
            reach = jnp.where(entered, jnp.exp(log2), 0.0)
            direct = jnp.where(left1, skip[x * HEADS + h], skip[x * HEADS + h + 1])
            y_out[j, :, at] = within + reach * across[:, at] + direct * xs.astype(F32)
        result(j).start()
        return token

    lax.fori_loop(0, NX, turn, 0)

    def finish(j, token):
        result(j).wait()
        return token

    lax.fori_loop(0, NX, finish, 0)


def scan_kernel(t_ref, *refs):
    e_out = refs[-1]
    parts, rows, _ = e_out.shape
    state = jnp.zeros(e_out.shape[1:], F32)
    for k in range(parts):
        e_out[k] = state.astype(BF16)
        if k < parts - 1:
            marks = t_ref[k, rows:].astype(F32)
            state = (marks[0:1] + marks[1:2]) * state + t_ref[k, :rows].astype(F32)


def gate_kernel(own, prev, nxt, far, y_hbm, bc_hbm, re_hbm, e_ref, gain_ref, *refs):
    *outs, gate, y_ref, query, re_ref, sems = refs[1:]
    x = lax.axis_index("x")
    copies = []
    for j in range(NX):
        b = j
        for src, dst in (
            (y_hbm.at[j], y_ref.at[b]),
            (bc_hbm.at[j, :, STATE:], query.at[b]),
            (re_hbm.at[j], re_ref.at[b]),
        ):
            copies.append(pltpu.make_async_copy(src, dst, sems.at[len(copies)]))
            copies[-1].start()
    gets = []
    for k, (by, src) in enumerate(((0, own), (3, prev), (1, nxt), (2, far))):
        gets.append(pltpu.make_async_copy(src, gate.at[around(x, by)], sems.at[12 + k]))
        gets[-1].start()
    for get in gets:
        get.wait()
    gain = gain_ref[:, lanes(x, WIDTH)]
    left = lax.broadcasted_iota(jnp.int32, (SPAN, 128), 1) < HEAD_DIM
    for b, out in enumerate(outs):
        for copy in copies[3 * b : 3 * b + 3]:
            copy.wait()
        across = jnp.dot(query[b], e_ref[...], preferred_element_type=F32)
        reach = re_ref[b]
        for pair in range(HEADS // 2):
            cols = slice(pair * 128, pair * 128 + 128)
            h = 2 * pair
            reach2 = jnp.where(left, reach[:, h : h + 1], reach[:, h + 1 : h + 2])
            g = gate[b, :, cols].astype(F32)
            v = (y_ref[b, :, cols] + reach2 * across[:, cols]) * (g * sigmoid(g))
            out[:, cols] = (v * gain[:, cols]).astype(BF16)


def product_kernel(*refs):
    gain_ref, w_ref = refs[8:10]
    send, kept, left = refs[-3:]
    x, c = lax.axis_index("x"), lax.axis_index("c")
    order = (x, around(x, 3), around(x, 1), around(x, 2))
    for k, ref in enumerate(refs[:8]):
        left[k // 4 * SPAN : k // 4 * SPAN + SPAN, lanes(order[k % 4], WIDTH)] = ref[...]
    plain = left[...] * (1.0 / gain_ref[...]).astype(BF16)
    ones = jnp.ones((NX * WIDTH, 128), BF16)
    mean = jnp.dot(plain * plain, ones, preferred_element_type=F32) * (1.0 / (NX * WIDTH))
    scale = lax.rsqrt(mean + 1e-05)
    scale = jnp.concatenate([scale, scale], axis=1)
    for core, out in ((1 - c, send), (c, kept)):
        for yy in range(0, NY, 2):
            w = jnp.concatenate([w_ref[2 * yy + core], w_ref[2 * yy + 2 + core]], axis=1)
            acc = jnp.dot(left[...], w, preferred_element_type=F32)
            acc = (acc * scale).astype(out.dtype)
            out[yy] = acc[:, :128]
            out[yy + 1] = acc[:, 128:]


def hold_kernel(w_any, after, out, sem):
    copy = pltpu.make_async_copy(w_any, out, sem)
    copy.start()
    copy.wait()


def cores_kernel(kept, got, to_next, to_prev, to_far, mine):
    y = lax.axis_index("y")
    for by, out in ((1, to_next), (3, to_prev), (2, to_far), (0, mine)):
        q = around(y, by)
        out[...] = (kept[q] + got[q].astype(F32)).astype(out.dtype)


def rows_kernel(a0, a1, a2, a3, b0, b1, b2, b3, own, to_next, to_prev, to_far, whole):
    x = lax.axis_index("x")
    first = a0[...] + a1[...].astype(F32) + a2[...].astype(F32) + a3[...].astype(F32)
    second = b0[...] + b1[...].astype(F32) + b2[...].astype(F32) + b3[...].astype(F32)
    whole[0] = first[:SPAN]
    whole[1] = first[SPAN:]
    whole[2] = second[:SPAN]
    whole[3] = second[SPAN:]
    for by, out in ((0, own), (1, to_next), (3, to_prev), (2, to_far)):
        out[...] = whole[around(x, by)].astype(BF16)


def place_kernel(own, prev, nxt, far, out):
    x = lax.axis_index("x")
    for by, got in ((0, own), (3, prev), (1, nxt), (2, far)):
        out[:, lanes(around(x, by), 128)] = got[...]


def on_device(
    x_in, bc_in, gate_in, dt_raw, decay_rate, skip_gain, conv_x, conv_bc, norm_gain, out_weight, lengths
):
    nz = lax.axis_size("z")
    bc = bc_in.reshape(SPAN, BC)
    w_all = lax.all_gather(out_weight, "z", axis=0)

    piece = ((SPAN + 16, BC), BF16)
    quarter = ((SPAN, WIDTH), BF16)
    edge = ((16, WIDE), BF16)
    packed = call(
        pack_kernel, "hhh", (x_in, bc, dt_raw.T), [piece] * 4 + [quarter] * 4 + [edge] * 4,
        [pltpu.VMEM((4 * HEADS, SPAN), F32), pltpu.SemaphoreType.DMA((17,))],
        nbytes=6 << 20,
    )

    def spread_out(to_next, to_prev, to_far, own):
        return own, shift(to_next, "x", 1), shift(to_prev, "x", -1), shift(to_far, "x", 2)

    def behind(v, k):
        return lax.ppermute(v, ("z", "x"), [((z - 1) * NX + NX - 1, z * NX + k) for z in range(1, nz)])

    bcs = spread_out(*packed[0:4])
    xs_in = spread_out(*packed[4:8])
    halo = [behind(e, k) for k, e in enumerate(packed[8:12])]
    far = xs_in[3]
    g_own, g_next, g_prev, g_far = call(
        split_kernel, "ha", (gate_in, far), [quarter] * 4, [pltpu.SemaphoreType.DMA((4,))],
        nbytes=2 << 20,
    )
    gates = (g_own, shift(g_next, "x", 1), shift(g_prev, "x", -1), shift(g_far, "x", 2))

    gain = norm_gain[None, :]
    rows = STATE // nz
    blocks_bc = pltpu.VMEM((NX, SPAN, BC), BF16)
    blocks_cols = pltpu.VMEM((NX, SPAN, 128), F32)
    blocks_rows = pltpu.VMEM((NX, 2 * HEADS, SPAN), F32)
    bcv, cols, lines, reach, total = call(
        step_kernel, "ss" + "v" * 9,
        (lengths, decay_rate, *halo, *bcs, conv_bc),
        [
            ((NX, SPAN, BC), BF16),
            ((NX, SPAN, 128), F32),
            ((NX, 2 * HEADS, SPAN), F32),
            ((NX, SPAN, 128), F32),
            ((8, 128), F32),
        ],
        [
            pltpu.VMEM((NX, SPAN + 16, BC), BF16),
            pltpu.VMEM((SPAN + 8, BC), F32),
            blocks_bc, blocks_cols, blocks_rows, blocks_cols,
            pltpu.SemaphoreType.DMA((4, NX)),
        ],
        flops=2 << 30, nbytes=8 << 20, places="hhhhv",
    )
    xs, carry, sums = call(
        state_kernel, "s" + "v" * 12,
        (lengths, *xs_in, *halo, conv_x, bcv, cols, total),
        [
            ((NX, SPAN, WIDTH), BF16),
            ((NX, STATE, WIDTH), BF16),
            ((nz, rows + 16, WIDTH), BF16),
        ],
        [
            pltpu.VMEM((NX, SPAN, WIDTH), BF16),
            pltpu.VMEM((SPAN + 8, WIDTH), F32),
            pltpu.VMEM((STATE, WIDTH), F32),
            pltpu.VMEM((SPAN, WIDTH), BF16),
            blocks_bc,
            blocks_bc,
            pltpu.SemaphoreType.DMA((2, NX)),
        ],
        flops=3 << 30, nbytes=10 << 20, places="hhv",
    )
    spread = lax.all_to_all(sums, "z", 0, 0, tiled=True)
    (mine,) = call(scan_kernel, "v", (spread,), [((nz, rows, WIDTH), BF16)], nbytes=1 << 20)
    (y_loc,) = call(
        within_kernel, "sshhhhhaaaa", (lengths, skip_gain, xs, bcv, cols, lines, carry, mine, *gates[1:]),
        [((NX, SPAN, WIDTH), F32)],
        [
            pltpu.VMEM((SPAN, SPAN), F32),
            blocks_bc, blocks_bc, blocks_cols, blocks_rows, blocks_bc,
            pltpu.VMEM((NX, SPAN, WIDTH), F32),
            pltpu.SemaphoreType.DMA((6, NX)),
        ],
        flops=6 << 30, nbytes=16 << 20, places="h",
    )
    enter = lax.all_to_all(mine, "z", 0, 0, tiled=True).reshape(STATE, WIDTH)

    halves = []
    v = call(
        gate_kernel, "aaaahhhvva", (*gates, y_loc, bcv, reach, enter, gain, w_all),
        [quarter] * NX,
        [
            pltpu.VMEM((NX, SPAN, WIDTH), BF16),
            pltpu.VMEM((NX, SPAN, WIDTH), F32),
            pltpu.VMEM((NX, SPAN, STATE), BF16),
            pltpu.VMEM((NX, SPAN, 128), F32),
            pltpu.SemaphoreType.DMA((16,)),
        ],
        flops=2 << 30, nbytes=6 << 20,
    )
    parts = []
    for k, o in enumerate(v):
        a, b = shift(o, "x", 1), shift(o, "x", -1)
        parts += [o, a, b, shift(a, "x", 1) if k % 2 == 0 else shift(b, "x", -1)]
    gathered = (parts[:8], parts[8:])
    (w_near,) = call(
        hold_kernel, "aa", (w_all, v[-1]), [((nz, NX * WIDTH, 128), BF16)],
        [pltpu.SemaphoreType.DMA(())], nbytes=1 << 20, vmem=SMALL,
    )
    after = tuple(parts[k] for k in (9, 10, 11, 13, 14, 15))
    for parts in gathered:
        send, kept = call(
            product_kernel, "v" * 10 + "a" * len(after), (*parts, gain, w_near, *after),
            [((NY, 2 * SPAN, 128), BF16), ((NY, 2 * SPAN, 128), F32)],
            [
                pltpu.VMEM((2 * SPAN, NX * WIDTH), BF16),
            ],
            flops=3 << 30, nbytes=8 << 20, vmem=SMALL,
        )
        got = shift(send, "c", 1)
        part = ((2 * SPAN, 128), BF16)
        y_next, y_prev, y_far, mine = call(
            cores_kernel, "vv", (kept, got), [part] * 3 + [((2 * SPAN, 128), F32)], nbytes=2 << 20, vmem=SMALL
        )
        after = ()
        halves += [mine, shift(y_next, "y", 1), shift(y_prev, "y", -1), shift(y_far, "y", 2)]
    tile = ((SPAN, 128), BF16)
    own, to_next, to_prev, to_far = call(
        rows_kernel, "v" * 8, halves, [tile] * 4, [pltpu.VMEM((NX, SPAN, 128), F32)], nbytes=2 << 20, vmem=SMALL
    )
    (mixed,) = call(
        place_kernel, "vvvv",
        (own, shift(to_next, "x", 1), shift(to_prev, "x", -1), shift(to_far, "x", 2)),
        [((SPAN, NX * 128), BF16)], nbytes=1 << 20, vmem=SMALL,
    )
    return mixed


def solution(mesh):
    seq, tp = ("z", "x"), ("y", "c")
    fine = Mesh(mesh.devices.reshape(mesh.devices.shape[0] // NX, NX, NY, 2), seq + tp)
    in_specs = (
        P(seq, tp),
        P(seq, tp, None),
        P(seq, tp),
        P(seq, tp),
        P(tp),
        P(tp),
        P(None, tp),
        P(None, tp, None),
        P(tp),
        P(tp, seq),
        P(),
    )
    return jax.shard_map(
        on_device, mesh=fine, in_specs=in_specs, out_specs=P(seq, tp), check_vma=False
    )
```

```python
import jax
import jax.numpy as jnp
from jax import lax
from jax.experimental import pallas as pl
from jax.experimental.pallas import tpu as pltpu
from jax.sharding import Mesh, PartitionSpec as P

SPAN = 256
NX = 4
NY = 4
HEADS = 8
HEAD_DIM = 64
WIDTH = HEADS * HEAD_DIM
STATE = 256
BC = 2 * STATE
WIDE = WIDTH + BC
F32 = jnp.float32
BF16 = jnp.bfloat16
LARGE = 60 * 1024 * 1024
SMALL = 20 * 1024 * 1024
SPECS = {
    "v": pl.BlockSpec(memory_space=pltpu.VMEM),
    "s": pl.BlockSpec(memory_space=pltpu.SMEM),
    "a": pl.BlockSpec(memory_space=pl.ANY),
    "h": pl.BlockSpec(memory_space=pl.ANY),
}


def call(kernel, spaces, args, outs, scratch=(), flops=0, nbytes=0, places=None, vmem=LARGE):
    return pl.pallas_call(
        kernel,
        in_specs=[SPECS[s] for s in spaces],
        out_specs=tuple(SPECS[s] for s in places or "v" * len(outs)),
        out_shape=tuple(jax.ShapeDtypeStruct(s, d) for s, d in outs),
        scratch_shapes=list(scratch),
        compiler_params=pltpu.CompilerParams(vmem_limit_bytes=vmem),
        cost_estimate=pl.CostEstimate(flops=flops, bytes_accessed=nbytes, transcendentals=0),
    )(*args)


def shift(v, axis, by):
    n = lax.axis_size(axis)
    return lax.ppermute(v, axis, [(i, (i + by) % n) for i in range(n)])


def around(v, by):
    return lax.rem(v + by, 4)


def sigmoid(v):
    return 0.5 * jnp.tanh(0.5 * v) + 0.5


def lanes(q, width):
    return pl.ds(pl.multiple_of(q * width, width), width)


def three_parts(v):
    hi = v.astype(BF16).astype(F32)
    mid = (v - hi).astype(BF16).astype(F32)
    return hi, mid, (v - hi - mid).astype(BF16).astype(F32)


def first_finder(lengths):
    s1 = lengths[0]
    s2 = s1 + lengths[1]
    s3 = s2 + lengths[2]
    return lambda t: jnp.where(t >= s3, s3, jnp.where(t >= s2, s2, jnp.where(t >= s1, s1, 0)))


def pack_kernel(x_any, bc_any, dt_any, *refs):
    bcs, xs, edges = refs[0:4], refs[4:8], refs[8:12]
    turned, sems = refs[12:]
    x = lax.axis_index("x")
    get_dt = pltpu.make_async_copy(dt_any, turned, sems.at[0])
    get_dt.start()
    copies = []

    def start(src, dst):
        copy = pltpu.make_async_copy(src, dst, sems.at[len(copies) + 1])
        copy.start()
        copies.append(copy)

    order = (1, 3, 2, 0)
    for out in bcs:
        start(bc_any, out.at[:SPAN, :])
    for by, out in zip(order, xs):
        start(x_any.at[:, lanes(around(x, by), WIDTH)], out)
    for q, out in enumerate(edges):
        start(x_any.at[SPAN - 16 :, q * WIDTH : (q + 1) * WIDTH], out.at[:, :WIDTH])
        start(bc_any.at[SPAN - 16 :, :], out.at[:, WIDTH:])
    get_dt.wait()
    for by, out in zip(order, bcs):
        rows = turned[pl.ds(pl.multiple_of(around(x, by) * HEADS, HEADS), HEADS), :]
        hi, mid, low = three_parts(rows)
        upper = jnp.concatenate([hi, mid], axis=1)
        lower = jnp.concatenate([low, jnp.zeros_like(low)], axis=1)
        out[SPAN:, :] = jnp.concatenate([upper, lower], axis=0).astype(BF16)
    for copy in copies:
        copy.wait()


def split_kernel(g_any, after, own, to_next, to_prev, to_far, sems):
    x = lax.axis_index("x")
    copies = []
    for k, (by, out) in enumerate(((0, own), (1, to_next), (3, to_prev), (2, to_far))):
        copies.append(pltpu.make_async_copy(g_any.at[:, lanes(around(x, by), WIDTH)], out, sems.at[k]))
        copies[-1].start()
    for copy in copies:
        copy.wait()


def convolve(ext, tap, pos, at):
    cols = slice(at, at + 128)
    acc = tap(3, at) * ext[8 : 8 + SPAN, cols]
    for back in (1, 2, 3):
        term = tap(3 - back, at) * ext[8 - back : 8 - back + SPAN, cols]
        acc = acc + jnp.where(pos >= back, term, 0.0)
    return (acc * sigmoid(acc)).astype(BF16)


def step_kernel(
    lengths, decay, h0, h1, h2, h3, own, prev, nxt, far, cb_ref,
    bc_hbm, cols_hbm, rows_hbm, re_hbm, total_out,
    pay, ext, bc_out, cols_out, rows_out, re_out, sems,
):
    def outgoing(j):
        pairs = ((bc_out, bc_hbm), (cols_out, cols_hbm), (rows_out, rows_hbm), (re_out, re_hbm))
        return [
            pltpu.make_async_copy(src.at[j], dst.at[j], sems.at[k, j])
            for k, (src, dst) in enumerate(pairs)
        ]

    x = lax.axis_index("x")
    base = lax.axis_index("z") * (NX * SPAN)
    first_of = first_finder(lengths)
    for by, src in ((0, own), (3, prev), (1, nxt), (2, far)):
        pay[around(x, by)] = src[...]
    cut = slice(WIDTH, WIDTH + BC)
    ext[0:8] = (
        h0[8:16, cut].astype(F32)
        + h1[8:16, cut].astype(F32)
        + h2[8:16, cut].astype(F32)
        + h3[8:16, cut].astype(F32)
    )
    head = lax.broadcasted_iota(jnp.int32, (HEADS, SPAN), 0)
    rates = jnp.zeros((HEADS, SPAN), F32)
    for h in range(HEADS):
        rates = jnp.where(head == h, decay[x * HEADS + h], rates)
    raw = []
    for j in range(NX):
        packed = pay[j, SPAN:, :].astype(F32)
        raw.append(packed[:HEADS, :SPAN] + packed[:HEADS, SPAN:] + packed[HEADS:, :SPAN])
    raw = jnp.concatenate(raw, axis=0)
    step = jnp.maximum(raw, 0.0) + jnp.log1p(jnp.exp(-jnp.abs(raw)))
    rate = -jnp.concatenate([rates] * NX, axis=0) * step
    parts = jnp.concatenate([*three_parts(rate), jnp.zeros_like(rate)], axis=0).astype(BF16)
    wide_s = lax.broadcasted_iota(jnp.int32, (SPAN, SPAN), 0)
    wide_t = lax.broadcasted_iota(jnp.int32, (SPAN, SPAN), 1)
    upper = jnp.where(wide_s <= wide_t, 1.0, 0.0).astype(BF16)
    sums = jnp.dot(parts, upper, preferred_element_type=F32)
    n = NX * HEADS
    logd = sums[:n] + sums[n : 2 * n] + sums[2 * n : 3 * n]
    row = lax.broadcasted_iota(jnp.int32, (SPAN, 128), 0)
    lane1 = lax.broadcasted_iota(jnp.int32, (1, 128), 1)
    before = jnp.zeros((1, 128), F32)
    for j in range(NX):
        at = slice(j * HEADS, (j + 1) * HEADS)
        both = jnp.concatenate([logd[at], step[at]], axis=0)
        rows_out[j] = both
        cols = jnp.transpose(
            jnp.concatenate([both, jnp.zeros((128 - 2 * HEADS, SPAN), F32)], axis=0)
        )
        cols_out[j] = cols
        first = first_of(base + j * SPAN + row)
        re_out[j] = jnp.where(first < base, jnp.exp(jnp.minimum(cols + before, 0.0)), 0.0)
        before = before + jnp.where(lane1 < HEADS, cols[SPAN - 1 : SPAN, :], 0.0)
    total_out[...] = jnp.broadcast_to(before, total_out.shape)

    def turn(j, token):
        @pl.when(j > 0)
        def _():
            ext[0:8] = ext[SPAN : SPAN + 8]

        ext[8:] = pay[j, :SPAN, :].astype(F32)
        place = base + j * SPAN + row
        pos = place - first_of(place)
        for part in range(BC // 128):
            at = part * 128
            bc_out[j, :, at : at + 128] = convolve(
                ext, lambda k, at: cb_ref[k][:, at : at + 128], pos, at
            )
        for copy in outgoing(j):
            copy.start()
        return token

    lax.fori_loop(0, NX, turn, 0, unroll=True)

    def finish(j, token):
        for copy in outgoing(j):
            copy.wait()
        return token

    lax.fori_loop(0, NX, finish, 0)


def state_kernel(
    lengths, own, prev, nxt, far, h0, h1, h2, h3, cw_ref, bc_ref, cols_ref, total_ref, w_any,
    xs_hbm, carry_hbm, w_hbm, t_out,
    pay, ext, carry, weighted, xs_out, carry_out, w_held, sems, w_sems,
):
    get_w = pltpu.make_async_copy(w_any, w_held, w_sems.at[0])
    put_w = pltpu.make_async_copy(w_held, w_hbm, w_sems.at[1])
    get_w.start()

    def outgoing(j):
        pairs = ((xs_out, xs_hbm), (carry_out, carry_hbm))
        return [
            pltpu.make_async_copy(src.at[j], dst.at[j], sems.at[k, j])
            for k, (src, dst) in enumerate(pairs)
        ]

    x = lax.axis_index("x")
    base = lax.axis_index("z") * (NX * SPAN)
    first_of = first_finder(lengths)
    for by, src in ((0, own), (3, prev), (1, nxt), (2, far)):
        pay[around(x, by)] = src[...]
    ext[0:8] = (
        h0[8:16, :WIDTH].astype(F32)
        + h1[8:16, :WIDTH].astype(F32)
        + h2[8:16, :WIDTH].astype(F32)
        + h3[8:16, :WIDTH].astype(F32)
    )
    carry[...] = jnp.zeros_like(carry)
    taps = cw_ref[:, lanes(x, WIDTH)]
    row = lax.broadcasted_iota(jnp.int32, (SPAN, 128), 0)
    left = lax.broadcasted_iota(jnp.int32, (SPAN, 128), 1) < HEAD_DIM
    left1 = lax.broadcasted_iota(jnp.int32, (1, 128), 1) < HEAD_DIM

    def turn(j, token):
        start = base + j * SPAN

        @pl.when(j > 0)
        def _():
            ext[0:8] = ext[SPAN : SPAN + 8]

        ext[8:] = pay[j].astype(F32)
        place = start + row
        pos = place - first_of(place)
        first_end = first_of(start + SPAN - 1)
        keep = place >= first_end
        carried = jnp.where(first_end < start, 1.0, 0.0)
        cols = cols_ref[j]
        end = cols[SPAN - 1 : SPAN, :]
        decays = []
        for pair in range(HEADS // 2):
            at = slice(pair * 128, pair * 128 + 128)
            h = 2 * pair
            xs = convolve(ext, lambda k, at: taps[k : k + 1, at : at + 128], pos, pair * 128)
            xs_out[j, :, at] = xs
            log2 = jnp.where(left, cols[:, h : h + 1], cols[:, h + 1 : h + 2])
            s = HEADS + h
            step2 = jnp.where(left, cols[:, s : s + 1], cols[:, s + 1 : s + 2])
            end2 = jnp.where(left1, end[:, h : h + 1], end[:, h + 1 : h + 2])
            inputs = jnp.where(keep, jnp.exp(end2 - log2) * step2, 0.0) * xs.astype(F32)
            weighted[:, at] = inputs.astype(BF16)
            decays.append(jnp.exp(end2) * carried)
        states = lax.dot_general(
            bc_ref[j, :, :STATE], weighted[...], (((0,), (0,)), ((), ())), preferred_element_type=F32
        )
        state = carry[...]
        carry_out[j] = state.astype(BF16)
        carry[...] = jnp.concatenate(decays, axis=1) * state + states
        for copy in outgoing(j):
            copy.start()
        return token

    lax.fori_loop(0, NX, turn, 0, unroll=True)
    get_w.wait()
    put_w.start()
    last = first_of(base + NX * SPAN - 1)
    whole = jnp.where(last < base, jnp.exp(total_ref[0:1, :]), 0.0)
    hi = whole.astype(BF16).astype(F32)
    parts, rows, _ = t_out.shape
    which = lax.broadcasted_iota(jnp.int32, (rows, 128), 0)
    marks = jnp.where(which == 0, hi, jnp.where(which == 1, whole - hi, 0.0)).astype(BF16)
    for k in range(parts):
        t_out[k, :, :WIDTH] = carry[k * rows : (k + 1) * rows].astype(BF16)
        t_out[k, :, WIDTH:] = marks

    def finish(j, token):
        for copy in outgoing(j):
            copy.wait()
        return token

    lax.fori_loop(0, NX, finish, 0)
    put_w.wait()


def within_kernel(
    lengths, skip, xs_hbm, bc_hbm, cols_hbm, rows_hbm, carry_hbm, *refs
):
    y_hbm, gram, xs_ref, bc_ref, cols_ref, rows_ref, carry_ref, y_out, sems = refs[-9:]

    def incoming(j):
        pairs = (
            (xs_hbm, xs_ref),
            (bc_hbm, bc_ref),
            (cols_hbm, cols_ref),
            (rows_hbm, rows_ref),
            (carry_hbm, carry_ref),
        )
        return [
            pltpu.make_async_copy(src.at[j], dst.at[j], sems.at[k, j])
            for k, (src, dst) in enumerate(pairs)
        ]

    def result(j):
        return pltpu.make_async_copy(y_out.at[j], y_hbm.at[j], sems.at[5, j])

    def begin(j, token):
        for copy in incoming(j):
            copy.start()
        return token

    lax.fori_loop(0, NX, begin, 0)
    x = lax.axis_index("x")
    base = lax.axis_index("z") * (NX * SPAN)
    first_of = first_finder(lengths)
    half = SPAN // 2

    def turn(j, token):
        for copy in incoming(j):
            copy.wait()
        start = base + j * SPAN
        row = lax.broadcasted_iota(jnp.int32, (SPAN, 128), 0)
        lane = lax.broadcasted_iota(jnp.int32, (SPAN, 128), 1)
        left = lane < HEAD_DIM
        left1 = lax.broadcasted_iota(jnp.int32, (1, 128), 1) < HEAD_DIM
        entered = first_of(start + row) < start
        keys = bc_ref[j, :, :STATE]
        query = bc_ref[j, :, STATE:]
        dots = lax.dot_general(query, keys, (((1,), (1,)), ((), ())), preferred_element_type=F32)
        wide_t = lax.broadcasted_iota(jnp.int32, (SPAN, SPAN), 0)
        wide_s = lax.broadcasted_iota(jnp.int32, (SPAN, SPAN), 1)
        wide_first = first_of(start + wide_t)
        gram[...] = jnp.where((wide_s <= wide_t) & (start + wide_s >= wide_first), dots, 0.0)
        across = jnp.dot(query, carry_ref[j], preferred_element_type=F32)
        cols = cols_ref[j]
        rows = rows_ref[j]
        for pair in range(HEADS // 2):
            at = slice(pair * 128, pair * 128 + 128)
            xs = xs_ref[j, :, at]
            tops, bottoms = [], []
            for h in (2 * pair, 2 * pair + 1):
                column = cols[:, h : h + 1]
                log_row = rows[h : h + 1, :]
                weight = rows[HEADS + h : HEADS + h + 1, :]
                top = jnp.exp(jnp.minimum(column[:half] - log_row[:, :half], 0.0)) * (
                    gram[:half, :half] * weight[:, :half]
                )
                bottom = jnp.exp(jnp.minimum(column[half:] - log_row, 0.0)) * (
                    gram[half:, :] * weight
                )
                tops.append(jnp.dot(top.astype(BF16), xs[:half], preferred_element_type=F32))
                bottoms.append(jnp.dot(bottom.astype(BF16), xs, preferred_element_type=F32))
            within = jnp.concatenate(
                [
                    jnp.where(left[:half], tops[0], tops[1]),
                    jnp.where(left[half:], bottoms[0], bottoms[1]),
                ],
                axis=0,
            )
            h = 2 * pair
            log2 = jnp.where(left, cols[:, h : h + 1], cols[:, h + 1 : h + 2])
            reach = jnp.where(entered, jnp.exp(log2), 0.0)
            direct = jnp.where(left1, skip[x * HEADS + h], skip[x * HEADS + h + 1])
            y_out[j, :, at] = within + reach * across[:, at] + direct * xs.astype(F32)
        result(j).start()
        return token

    lax.fori_loop(0, NX, turn, 0)

    def finish(j, token):
        result(j).wait()
        return token

    lax.fori_loop(0, NX, finish, 0)


def scan_kernel(t_ref, e_out):
    parts, rows, _ = e_out.shape
    left1 = lax.broadcasted_iota(jnp.int32, (1, 128), 1) < HEAD_DIM
    state = jnp.zeros(e_out.shape[1:], F32)
    for k in range(parts):
        e_out[k] = state.astype(BF16)
        if k < parts - 1:
            marks = t_ref[k, :16, WIDTH:].astype(F32)
            whole = marks[0:1] + marks[1:2]
            spread = jnp.concatenate(
                [
                    jnp.where(left1, whole[:, h : h + 1], whole[:, h + 1 : h + 2])
                    for h in range(0, HEADS, 2)
                ],
                axis=1,
            )
            state = spread * state + t_ref[k, :, :WIDTH].astype(F32)


def gate_kernel(own, prev, nxt, far, y_hbm, bc_hbm, re_hbm, e_ref, gain_ref, *refs):
    *outs, gate, y_ref, query, re_ref, enter, sems = refs
    x = lax.axis_index("x")
    gets = [pltpu.make_async_copy(e_ref, enter, sems.at[16])]
    gets[0].start()
    copies = []
    for j in range(NX):
        b = j
        for src, dst in (
            (y_hbm.at[j], y_ref.at[b]),
            (bc_hbm.at[j, :, STATE:], query.at[b]),
            (re_hbm.at[j], re_ref.at[b]),
        ):
            copies.append(pltpu.make_async_copy(src, dst, sems.at[len(copies)]))
            copies[-1].start()
    for k, (by, src) in enumerate(((0, own), (3, prev), (1, nxt), (2, far))):
        gets.append(pltpu.make_async_copy(src, gate.at[around(x, by)], sems.at[12 + k]))
        gets[-1].start()
    for get in gets:
        get.wait()
    gain = gain_ref[:, lanes(x, WIDTH)]
    left = lax.broadcasted_iota(jnp.int32, (SPAN, 128), 1) < HEAD_DIM
    for b, out in enumerate(outs):
        for copy in copies[3 * b : 3 * b + 3]:
            copy.wait()
        across = jnp.dot(query[b], enter[...], preferred_element_type=F32)
        reach = re_ref[b]
        for pair in range(HEADS // 2):
            cols = slice(pair * 128, pair * 128 + 128)
            h = 2 * pair
            reach2 = jnp.where(left, reach[:, h : h + 1], reach[:, h + 1 : h + 2])
            g = gate[b, :, cols].astype(F32)
            v = (y_ref[b, :, cols] + reach2 * across[:, cols]) * (g * sigmoid(g))
            out[:, cols] = (v * gain[:, cols]).astype(BF16)


def product_kernel(*refs):
    gain_ref, w_ref = refs[8:10]
    send, kept, left = refs[-3:]
    x, c = lax.axis_index("x"), lax.axis_index("c")
    order = (x, around(x, 3), around(x, 1), around(x, 2))
    for k, ref in enumerate(refs[:8]):
        left[k // 4 * SPAN : k // 4 * SPAN + SPAN, lanes(order[k % 4], WIDTH)] = ref[...]
    plain = left[...] * (1.0 / gain_ref[...]).astype(BF16)
    ones = jnp.ones((NX * WIDTH, 128), BF16)
    mean = jnp.dot(plain * plain, ones, preferred_element_type=F32) * (1.0 / (NX * WIDTH))
    scale = lax.rsqrt(mean + 1e-05)
    scale = jnp.concatenate([scale, scale], axis=1)
    for core, out in ((1 - c, send), (c, kept)):
        for yy in range(0, NY, 2):
            w = jnp.concatenate([w_ref[2 * yy + core], w_ref[2 * yy + 2 + core]], axis=1)
            acc = jnp.dot(left[...], w, preferred_element_type=F32)
            acc = (acc * scale).astype(out.dtype)
            out[yy] = acc[:, :128]
            out[yy + 1] = acc[:, 128:]


def hold_kernel(w_any, after, out, sem):
    copy = pltpu.make_async_copy(w_any, out, sem)
    copy.start()
    copy.wait()


def cores_kernel(kept, got, to_next, to_prev, to_far, mine):
    y = lax.axis_index("y")
    for by, out in ((1, to_next), (3, to_prev), (2, to_far), (0, mine)):
        q = around(y, by)
        out[...] = (kept[q] + got[q].astype(F32)).astype(out.dtype)


def rows_kernel(a0, a1, a2, a3, b0, b1, b2, b3, own, to_next, to_prev, to_far, whole):
    x = lax.axis_index("x")
    first = a0[...] + a1[...].astype(F32) + a2[...].astype(F32) + a3[...].astype(F32)
    second = b0[...] + b1[...].astype(F32) + b2[...].astype(F32) + b3[...].astype(F32)
    whole[0] = first[:SPAN]
    whole[1] = first[SPAN:]
    whole[2] = second[:SPAN]
    whole[3] = second[SPAN:]
    for by, out in ((0, own), (1, to_next), (3, to_prev), (2, to_far)):
        out[...] = whole[around(x, by)].astype(BF16)


def place_kernel(own, prev, nxt, far, out):
    x = lax.axis_index("x")
    for by, got in ((0, own), (3, prev), (1, nxt), (2, far)):
        out[:, lanes(around(x, by), 128)] = got[...]


def on_device(
    x_in, bc_in, gate_in, dt_raw, decay_rate, skip_gain, conv_x, conv_bc, norm_gain, out_weight, lengths
):
    nz = lax.axis_size("z")
    bc = bc_in.reshape(SPAN, BC)

    piece = ((SPAN + 16, BC), BF16)
    quarter = ((SPAN, WIDTH), BF16)
    edge = ((16, WIDE), BF16)
    packed = call(
        pack_kernel, "hhh", (x_in, bc, dt_raw.T), [piece] * 4 + [quarter] * 4 + [edge] * 4,
        [pltpu.VMEM((4 * HEADS, SPAN), F32), pltpu.SemaphoreType.DMA((17,))],
        nbytes=6 << 20,
    )

    def spread_out(to_next, to_prev, to_far, own):
        return own, shift(to_next, "x", 1), shift(to_prev, "x", -1), shift(to_far, "x", 2)

    def behind(v, k):
        return lax.ppermute(v, ("z", "x"), [((z - 1) * NX + NX - 1, z * NX + k) for z in range(1, nz)])

    bcs = spread_out(*packed[0:4])
    xs_in = spread_out(*packed[4:8])
    halo = [behind(e, k) for k, e in enumerate(packed[8:12])]
    far = xs_in[3]
    g_own, g_next, g_prev, g_far = call(
        split_kernel, "ha", (gate_in, far), [quarter] * 4, [pltpu.SemaphoreType.DMA((4,))],
        nbytes=2 << 20,
    )
    gates = (g_own, shift(g_next, "x", 1), shift(g_prev, "x", -1), shift(g_far, "x", 2))

    gain = norm_gain[None, :]
    rows = STATE // nz
    blocks_bc = pltpu.VMEM((NX, SPAN, BC), BF16)
    blocks_cols = pltpu.VMEM((NX, SPAN, 128), F32)
    blocks_rows = pltpu.VMEM((NX, 2 * HEADS, SPAN), F32)
    bcv, cols, lines, reach, total = call(
        step_kernel, "ss" + "v" * 9,
        (lengths, decay_rate, *halo, *bcs, conv_bc),
        [
            ((NX, SPAN, BC), BF16),
            ((NX, SPAN, 128), F32),
            ((NX, 2 * HEADS, SPAN), F32),
            ((NX, SPAN, 128), F32),
            ((8, 128), F32),
        ],
        [
            pltpu.VMEM((NX, SPAN + 16, BC), BF16),
            pltpu.VMEM((SPAN + 8, BC), F32),
            blocks_bc, blocks_cols, blocks_rows, blocks_cols,
            pltpu.SemaphoreType.DMA((4, NX)),
        ],
        flops=2 << 30, nbytes=8 << 20, places="hhhhv",
    )
    xs, carry, weight, sums = call(
        state_kernel, "s" + "v" * 12 + "h",
        (lengths, *xs_in, *halo, conv_x, bcv, cols, total, out_weight),
        [
            ((NX, SPAN, WIDTH), BF16),
            ((NX, STATE, WIDTH), BF16),
            (out_weight.shape, BF16),
            ((nz, rows, WIDTH + 128), BF16),
        ],
        [
            pltpu.VMEM((NX, SPAN, WIDTH), BF16),
            pltpu.VMEM((SPAN + 8, WIDTH), F32),
            pltpu.VMEM((STATE, WIDTH), F32),
            pltpu.VMEM((SPAN, WIDTH), BF16),
            blocks_bc,
            blocks_bc,
            pltpu.VMEM(out_weight.shape, BF16),
            pltpu.SemaphoreType.DMA((2, NX)),
            pltpu.SemaphoreType.DMA((2,)),
        ],
        flops=3 << 30, nbytes=10 << 20, places="hhhv",
    )
    w_all = lax.all_gather(weight, "z", axis=0)
    spread = lax.all_to_all(sums, "z", 0, 0, tiled=True)
    (mine,) = call(scan_kernel, "v", (spread,), [((nz, rows, WIDTH), BF16)], nbytes=1 << 20)
    (y_loc,) = call(
        within_kernel, "sshhhhhaaaa", (lengths, skip_gain, xs, bcv, cols, lines, carry, mine, *gates[1:]),
        [((NX, SPAN, WIDTH), F32)],
        [
            pltpu.VMEM((SPAN, SPAN), F32),
            blocks_bc, blocks_bc, blocks_cols, blocks_rows, blocks_bc,
            pltpu.VMEM((NX, SPAN, WIDTH), F32),
            pltpu.SemaphoreType.DMA((6, NX)),
        ],
        flops=6 << 30, nbytes=16 << 20, places="h",
    )
    enter = lax.all_to_all(mine, "z", 0, 0, tiled=True).reshape(STATE, WIDTH)

    halves = []
    v = call(
        gate_kernel, "aaaahhhav", (*gates, y_loc, bcv, reach, enter, gain),
        [quarter] * NX,
        [
            pltpu.VMEM((NX, SPAN, WIDTH), BF16),
            pltpu.VMEM((NX, SPAN, WIDTH), F32),
            pltpu.VMEM((NX, SPAN, STATE), BF16),
            pltpu.VMEM((NX, SPAN, 128), F32),
            pltpu.VMEM((STATE, WIDTH), BF16),
            pltpu.SemaphoreType.DMA((17,)),
        ],
        flops=2 << 30, nbytes=6 << 20,
    )
    parts = []
    for k, o in enumerate(v):
        a, b = shift(o, "x", 1), shift(o, "x", -1)
        parts += [o, a, b, shift(a, "x", 1) if k % 2 == 0 else shift(b, "x", -1)]
    gathered = (parts[:8], parts[8:])
    (w_near,) = call(
        hold_kernel, "aa", (w_all, v[-1]), [((nz, NX * WIDTH, 128), BF16)],
        [pltpu.SemaphoreType.DMA(())], nbytes=1 << 20, vmem=SMALL,
    )
    after = tuple(parts[k] for k in (9, 10, 11, 13, 14, 15))
    for parts in gathered:
        send, kept = call(
            product_kernel, "v" * 10 + "a" * len(after), (*parts, gain, w_near, *after),
            [((NY, 2 * SPAN, 128), BF16), ((NY, 2 * SPAN, 128), F32)],
            [
                pltpu.VMEM((2 * SPAN, NX * WIDTH), BF16),
            ],
            flops=3 << 30, nbytes=8 << 20, vmem=SMALL,
        )
        got = shift(send, "c", 1)
        part = ((2 * SPAN, 128), BF16)
        y_next, y_prev, y_far, mine = call(
            cores_kernel, "vv", (kept, got), [part] * 3 + [((2 * SPAN, 128), F32)], nbytes=2 << 20, vmem=SMALL
        )
        after = ()
        halves += [mine, shift(y_next, "y", 1), shift(y_prev, "y", -1), shift(y_far, "y", 2)]
    tile = ((SPAN, 128), BF16)
    own, to_next, to_prev, to_far = call(
        rows_kernel, "v" * 8, halves, [tile] * 4, [pltpu.VMEM((NX, SPAN, 128), F32)], nbytes=2 << 20, vmem=SMALL
    )
    (mixed,) = call(
        place_kernel, "vvvv",
        (own, shift(to_next, "x", 1), shift(to_prev, "x", -1), shift(to_far, "x", 2)),
        [((SPAN, NX * 128), BF16)], nbytes=1 << 20, vmem=SMALL,
    )
    return mixed


def solution(mesh):
    seq, tp = ("z", "x"), ("y", "c")
    fine = Mesh(mesh.devices.reshape(mesh.devices.shape[0] // NX, NX, NY, 2), seq + tp)
    in_specs = (
        P(seq, tp),
        P(seq, tp, None),
        P(seq, tp),
        P(seq, tp),
        P(tp),
        P(tp),
        P(None, tp),
        P(None, tp, None),
        P(tp),
        P(tp, seq),
        P(),
    )
    return jax.shard_map(
        on_device, mesh=fine, in_specs=in_specs, out_specs=P(seq, tp), check_vma=False
    )
```

```python
import jax
import jax.numpy as jnp
from jax import lax
from jax.experimental import pallas as pl
from jax.experimental.pallas import tpu as pltpu
from jax.sharding import Mesh, PartitionSpec as P

SPAN = 256
NX = 4
NY = 4
HEADS = 8
HEAD_DIM = 64
WIDTH = HEADS * HEAD_DIM
STATE = 256
BC = 2 * STATE
WIDE = WIDTH + BC
F32 = jnp.float32
BF16 = jnp.bfloat16
LARGE = 60 * 1024 * 1024
SMALL = 20 * 1024 * 1024
SPECS = {
    "v": pl.BlockSpec(memory_space=pltpu.VMEM),
    "s": pl.BlockSpec(memory_space=pltpu.SMEM),
    "a": pl.BlockSpec(memory_space=pl.ANY),
    "h": pl.BlockSpec(memory_space=pl.ANY),
}


def call(kernel, spaces, args, outs, scratch=(), flops=0, nbytes=0, places=None, vmem=LARGE):
    return pl.pallas_call(
        kernel,
        in_specs=[SPECS[s] for s in spaces],
        out_specs=tuple(SPECS[s] for s in places or "v" * len(outs)),
        out_shape=tuple(jax.ShapeDtypeStruct(s, d) for s, d in outs),
        scratch_shapes=list(scratch),
        compiler_params=pltpu.CompilerParams(vmem_limit_bytes=vmem),
        cost_estimate=pl.CostEstimate(flops=flops, bytes_accessed=nbytes, transcendentals=0),
    )(*args)


def shift(v, axis, by):
    n = lax.axis_size(axis)
    return lax.ppermute(v, axis, [(i, (i + by) % n) for i in range(n)])


def around(v, by):
    return lax.rem(v + by, 4)


def sigmoid(v):
    return 0.5 * jnp.tanh(0.5 * v) + 0.5


def lanes(q, width):
    return pl.ds(pl.multiple_of(q * width, width), width)


def three_parts(v):
    hi = v.astype(BF16).astype(F32)
    mid = (v - hi).astype(BF16).astype(F32)
    return hi, mid, (v - hi - mid).astype(BF16).astype(F32)


def first_finder(lengths):
    s1 = lengths[0]
    s2 = s1 + lengths[1]
    s3 = s2 + lengths[2]
    return lambda t: jnp.where(t >= s3, s3, jnp.where(t >= s2, s2, jnp.where(t >= s1, s1, 0)))


def pack_kernel(x_any, bc_any, dt_any, *refs):
    bcs, xs, edges = refs[0:4], refs[4:8], refs[8:12]
    turned, sems = refs[12:]
    x = lax.axis_index("x")
    get_dt = pltpu.make_async_copy(dt_any, turned, sems.at[0])
    get_dt.start()
    copies = []

    def start(src, dst):
        copy = pltpu.make_async_copy(src, dst, sems.at[len(copies) + 1])
        copy.start()
        copies.append(copy)

    order = (1, 3, 2, 0)
    for out in bcs:
        start(bc_any, out.at[:SPAN, :])
    for by, out in zip(order, xs):
        start(x_any.at[:, lanes(around(x, by), WIDTH)], out)
    for q, out in enumerate(edges):
        start(x_any.at[SPAN - 16 :, q * WIDTH : (q + 1) * WIDTH], out.at[:, :WIDTH])
        start(bc_any.at[SPAN - 16 :, :], out.at[:, WIDTH:])
    get_dt.wait()
    for by, out in zip(order, bcs):
        rows = turned[pl.ds(pl.multiple_of(around(x, by) * HEADS, HEADS), HEADS), :]
        hi, mid, low = three_parts(rows)
        upper = jnp.concatenate([hi, mid], axis=1)
        lower = jnp.concatenate([low, jnp.zeros_like(low)], axis=1)
        out[SPAN:, :] = jnp.concatenate([upper, lower], axis=0).astype(BF16)
    for copy in copies:
        copy.wait()


def split_kernel(g_any, after, own, to_next, to_prev, to_far, sems):
    x = lax.axis_index("x")
    copies = []
    for k, (by, out) in enumerate(((0, own), (1, to_next), (3, to_prev), (2, to_far))):
        copies.append(pltpu.make_async_copy(g_any.at[:, lanes(around(x, by), WIDTH)], out, sems.at[k]))
        copies[-1].start()
    for copy in copies:
        copy.wait()


def convolve(ext, tap, pos, at):
    cols = slice(at, at + 128)
    acc = tap(3, at) * ext[8 : 8 + SPAN, cols]
    for back in (1, 2, 3):
        term = tap(3 - back, at) * ext[8 - back : 8 - back + SPAN, cols]
        acc = acc + jnp.where(pos >= back, term, 0.0)
    return (acc * sigmoid(acc)).astype(BF16)


def step_kernel(
    lengths, decay, h0, h1, h2, h3, own, prev, nxt, far, cb_ref,
    bc_hbm, cols_hbm, rows_hbm, re_hbm, total_out,
    pay, ext, bc_out, cols_out, rows_out, re_out, sems,
):
    def outgoing(j):
        pairs = ((bc_out, bc_hbm), (cols_out, cols_hbm), (rows_out, rows_hbm), (re_out, re_hbm))
        return [
            pltpu.make_async_copy(src.at[j], dst.at[j], sems.at[k, j])
            for k, (src, dst) in enumerate(pairs)
        ]

    x = lax.axis_index("x")
    base = lax.axis_index("z") * (NX * SPAN)
    first_of = first_finder(lengths)
    for by, src in ((0, own), (3, prev), (1, nxt), (2, far)):
        pay[around(x, by)] = src[...]
    cut = slice(WIDTH, WIDTH + BC)
    ext[0:8] = (
        h0[8:16, cut].astype(F32)
        + h1[8:16, cut].astype(F32)
        + h2[8:16, cut].astype(F32)
        + h3[8:16, cut].astype(F32)
    )
    head = lax.broadcasted_iota(jnp.int32, (HEADS, SPAN), 0)
    rates = jnp.zeros((HEADS, SPAN), F32)
    for h in range(HEADS):
        rates = jnp.where(head == h, decay[x * HEADS + h], rates)
    raw = []
    for j in range(NX):
        packed = pay[j, SPAN:, :].astype(F32)
        raw.append(packed[:HEADS, :SPAN] + packed[:HEADS, SPAN:] + packed[HEADS:, :SPAN])
    raw = jnp.concatenate(raw, axis=0)
    step = jnp.maximum(raw, 0.0) + jnp.log1p(jnp.exp(-jnp.abs(raw)))
    rate = -jnp.concatenate([rates] * NX, axis=0) * step
    parts = jnp.concatenate([*three_parts(rate), jnp.zeros_like(rate)], axis=0).astype(BF16)
    wide_s = lax.broadcasted_iota(jnp.int32, (SPAN, SPAN), 0)
    wide_t = lax.broadcasted_iota(jnp.int32, (SPAN, SPAN), 1)
    upper = jnp.where(wide_s <= wide_t, 1.0, 0.0).astype(BF16)
    sums = jnp.dot(parts, upper, preferred_element_type=F32)
    n = NX * HEADS
    logd = sums[:n] + sums[n : 2 * n] + sums[2 * n : 3 * n]
    row = lax.broadcasted_iota(jnp.int32, (SPAN, 128), 0)
    lane1 = lax.broadcasted_iota(jnp.int32, (1, 128), 1)
    before = jnp.zeros((1, 128), F32)
    for j in range(NX):
        at = slice(j * HEADS, (j + 1) * HEADS)
        both = jnp.concatenate([logd[at], step[at]], axis=0)
        rows_out[j] = both
        cols = jnp.transpose(
            jnp.concatenate([both, jnp.zeros((128 - 2 * HEADS, SPAN), F32)], axis=0)
        )
        cols_out[j] = cols
        first = first_of(base + j * SPAN + row)
        re_out[j] = jnp.where(first < base, jnp.exp(jnp.minimum(cols + before, 0.0)), 0.0)
        before = before + jnp.where(lane1 < HEADS, cols[SPAN - 1 : SPAN, :], 0.0)
    total_out[...] = jnp.broadcast_to(before, total_out.shape)

    def turn(j, token):
        @pl.when(j > 0)
        def _():
            ext[0:8] = ext[SPAN : SPAN + 8]

        ext[8:] = pay[j, :SPAN, :].astype(F32)
        place = base + j * SPAN + row
        pos = place - first_of(place)
        for part in range(BC // 128):
            at = part * 128
            bc_out[j, :, at : at + 128] = convolve(
                ext, lambda k, at: cb_ref[k][:, at : at + 128], pos, at
            )
        for copy in outgoing(j):
            copy.start()
        return token

    lax.fori_loop(0, NX, turn, 0, unroll=True)

    def finish(j, token):
        for copy in outgoing(j):
            copy.wait()
        return token

    lax.fori_loop(0, NX, finish, 0)


def state_kernel(
    lengths, own, prev, nxt, far, h0, h1, h2, h3, cw_ref, bc_ref, cols_ref, total_ref,
    xs_hbm, carry_hbm, t_out,
    pay, ext, carry, weighted, xs_out, carry_out, sems,
):

    def outgoing(j):
        pairs = ((xs_out, xs_hbm), (carry_out, carry_hbm))
        return [
            pltpu.make_async_copy(src.at[j], dst.at[j], sems.at[k, j])
            for k, (src, dst) in enumerate(pairs)
        ]

    x = lax.axis_index("x")
    base = lax.axis_index("z") * (NX * SPAN)
    first_of = first_finder(lengths)
    for by, src in ((0, own), (3, prev), (1, nxt), (2, far)):
        pay[around(x, by)] = src[...]
    ext[0:8] = (
        h0[8:16, :WIDTH].astype(F32)
        + h1[8:16, :WIDTH].astype(F32)
        + h2[8:16, :WIDTH].astype(F32)
        + h3[8:16, :WIDTH].astype(F32)
    )
    carry[...] = jnp.zeros_like(carry)
    taps = cw_ref[:, lanes(x, WIDTH)]
    row = lax.broadcasted_iota(jnp.int32, (SPAN, 128), 0)
    left = lax.broadcasted_iota(jnp.int32, (SPAN, 128), 1) < HEAD_DIM
    left1 = lax.broadcasted_iota(jnp.int32, (1, 128), 1) < HEAD_DIM

    def turn(j, token):
        start = base + j * SPAN

        @pl.when(j > 0)
        def _():
            ext[0:8] = ext[SPAN : SPAN + 8]

        ext[8:] = pay[j].astype(F32)
        place = start + row
        pos = place - first_of(place)
        first_end = first_of(start + SPAN - 1)
        keep = place >= first_end
        carried = jnp.where(first_end < start, 1.0, 0.0)
        cols = cols_ref[j]
        end = cols[SPAN - 1 : SPAN, :]
        decays = []
        for pair in range(HEADS // 2):
            at = slice(pair * 128, pair * 128 + 128)
            h = 2 * pair
            xs = convolve(ext, lambda k, at: taps[k : k + 1, at : at + 128], pos, pair * 128)
            xs_out[j, :, at] = xs
            log2 = jnp.where(left, cols[:, h : h + 1], cols[:, h + 1 : h + 2])
            s = HEADS + h
            step2 = jnp.where(left, cols[:, s : s + 1], cols[:, s + 1 : s + 2])
            end2 = jnp.where(left1, end[:, h : h + 1], end[:, h + 1 : h + 2])
            inputs = jnp.where(keep, jnp.exp(end2 - log2) * step2, 0.0) * xs.astype(F32)
            weighted[:, at] = inputs.astype(BF16)
            decays.append(jnp.exp(end2) * carried)
        states = lax.dot_general(
            bc_ref[j, :, :STATE], weighted[...], (((0,), (0,)), ((), ())), preferred_element_type=F32
        )
        state = carry[...]
        carry_out[j] = state.astype(BF16)
        carry[...] = jnp.concatenate(decays, axis=1) * state + states
        for copy in outgoing(j):
            copy.start()
        return token

    lax.fori_loop(0, NX, turn, 0, unroll=True)
    last = first_of(base + NX * SPAN - 1)
    whole = jnp.where(last < base, jnp.exp(total_ref[0:1, :]), 0.0)
    hi = whole.astype(BF16).astype(F32)
    parts, rows, _ = t_out.shape
    which = lax.broadcasted_iota(jnp.int32, (rows, 128), 0)
    marks = jnp.where(which == 0, hi, jnp.where(which == 1, whole - hi, 0.0)).astype(BF16)
    for k in range(parts):
        t_out[k, :, :WIDTH] = carry[k * rows : (k + 1) * rows].astype(BF16)
        t_out[k, :, WIDTH:] = marks

    def finish(j, token):
        for copy in outgoing(j):
            copy.wait()
        return token

    lax.fori_loop(0, NX, finish, 0)


def within_kernel(
    lengths, skip, xs_hbm, bc_hbm, cols_hbm, rows_hbm, carry_hbm, *refs
):
    y_hbm, gram, xs_ref, bc_ref, cols_ref, rows_ref, carry_ref, y_out, sems = refs[-9:]

    def incoming(j):
        pairs = (
            (xs_hbm, xs_ref),
            (bc_hbm, bc_ref),
            (cols_hbm, cols_ref),
            (rows_hbm, rows_ref),
            (carry_hbm, carry_ref),
        )
        return [
            pltpu.make_async_copy(src.at[j], dst.at[j], sems.at[k, j])
            for k, (src, dst) in enumerate(pairs)
        ]

    def result(j):
        return pltpu.make_async_copy(y_out.at[j], y_hbm.at[j], sems.at[5, j])

    def begin(j, token):
        for copy in incoming(j):
            copy.start()
        return token

    lax.fori_loop(0, NX, begin, 0)
    x = lax.axis_index("x")
    base = lax.axis_index("z") * (NX * SPAN)
    first_of = first_finder(lengths)
    half = SPAN // 2

    def turn(j, token):
        for copy in incoming(j):
            copy.wait()
        start = base + j * SPAN
        row = lax.broadcasted_iota(jnp.int32, (SPAN, 128), 0)
        lane = lax.broadcasted_iota(jnp.int32, (SPAN, 128), 1)
        left = lane < HEAD_DIM
        left1 = lax.broadcasted_iota(jnp.int32, (1, 128), 1) < HEAD_DIM
        entered = first_of(start + row) < start
        keys = bc_ref[j, :, :STATE]
        query = bc_ref[j, :, STATE:]
        dots = lax.dot_general(query, keys, (((1,), (1,)), ((), ())), preferred_element_type=F32)
        wide_t = lax.broadcasted_iota(jnp.int32, (SPAN, SPAN), 0)
        wide_s = lax.broadcasted_iota(jnp.int32, (SPAN, SPAN), 1)
        wide_first = first_of(start + wide_t)
        gram[...] = jnp.where((wide_s <= wide_t) & (start + wide_s >= wide_first), dots, 0.0)
        across = jnp.dot(query, carry_ref[j], preferred_element_type=F32)
        cols = cols_ref[j]
        rows = rows_ref[j]
        for pair in range(HEADS // 2):
            at = slice(pair * 128, pair * 128 + 128)
            xs = xs_ref[j, :, at]
            tops, bottoms = [], []
            for h in (2 * pair, 2 * pair + 1):
                column = cols[:, h : h + 1]
                log_row = rows[h : h + 1, :]
                weight = rows[HEADS + h : HEADS + h + 1, :]
                top = jnp.exp(jnp.minimum(column[:half] - log_row[:, :half], 0.0)) * (
                    gram[:half, :half] * weight[:, :half]
                )
                bottom = jnp.exp(jnp.minimum(column[half:] - log_row, 0.0)) * (
                    gram[half:, :] * weight
                )
                tops.append(jnp.dot(top.astype(BF16), xs[:half], preferred_element_type=F32))
                bottoms.append(jnp.dot(bottom.astype(BF16), xs, preferred_element_type=F32))
            within = jnp.concatenate(
                [
                    jnp.where(left[:half], tops[0], tops[1]),
                    jnp.where(left[half:], bottoms[0], bottoms[1]),
                ],
                axis=0,
            )
            h = 2 * pair
            log2 = jnp.where(left, cols[:, h : h + 1], cols[:, h + 1 : h + 2])
            reach = jnp.where(entered, jnp.exp(log2), 0.0)
            direct = jnp.where(left1, skip[x * HEADS + h], skip[x * HEADS + h + 1])
            y_out[j, :, at] = within + reach * across[:, at] + direct * xs.astype(F32)
        result(j).start()
        return token

    lax.fori_loop(0, NX, turn, 0)

    def finish(j, token):
        result(j).wait()
        return token

    lax.fori_loop(0, NX, finish, 0)


def scan_kernel(t_ref, e_out):
    parts, rows, _ = e_out.shape
    left1 = lax.broadcasted_iota(jnp.int32, (1, 128), 1) < HEAD_DIM
    state = jnp.zeros(e_out.shape[1:], F32)
    for k in range(parts):
        e_out[k] = state.astype(BF16)
        if k < parts - 1:
            marks = t_ref[k, :16, WIDTH:].astype(F32)
            whole = marks[0:1] + marks[1:2]
            spread = jnp.concatenate(
                [
                    jnp.where(left1, whole[:, h : h + 1], whole[:, h + 1 : h + 2])
                    for h in range(0, HEADS, 2)
                ],
                axis=1,
            )
            state = spread * state + t_ref[k, :, :WIDTH].astype(F32)


def gate_kernel(own, prev, nxt, far, y_hbm, bc_hbm, re_hbm, e_ref, gain_ref, *refs):
    *outs, gate, y_ref, query, re_ref, enter, sems = refs[1:]
    x = lax.axis_index("x")
    gets = [pltpu.make_async_copy(e_ref, enter, sems.at[16])]
    gets[0].start()
    copies = []
    for j in range(NX):
        b = j
        for src, dst in (
            (y_hbm.at[j], y_ref.at[b]),
            (bc_hbm.at[j, :, STATE:], query.at[b]),
            (re_hbm.at[j], re_ref.at[b]),
        ):
            copies.append(pltpu.make_async_copy(src, dst, sems.at[len(copies)]))
            copies[-1].start()
    for k, (by, src) in enumerate(((0, own), (3, prev), (1, nxt), (2, far))):
        gets.append(pltpu.make_async_copy(src, gate.at[around(x, by)], sems.at[12 + k]))
        gets[-1].start()
    for get in gets:
        get.wait()
    gain = gain_ref[:, lanes(x, WIDTH)]
    left = lax.broadcasted_iota(jnp.int32, (SPAN, 128), 1) < HEAD_DIM
    for b, out in enumerate(outs):
        for copy in copies[3 * b : 3 * b + 3]:
            copy.wait()
        across = jnp.dot(query[b], enter[...], preferred_element_type=F32)
        reach = re_ref[b]
        for pair in range(HEADS // 2):
            cols = slice(pair * 128, pair * 128 + 128)
            h = 2 * pair
            reach2 = jnp.where(left, reach[:, h : h + 1], reach[:, h + 1 : h + 2])
            g = gate[b, :, cols].astype(F32)
            v = (y_ref[b, :, cols] + reach2 * across[:, cols]) * (g * sigmoid(g))
            out[:, cols] = (v * gain[:, cols]).astype(BF16)


def product_kernel(*refs):
    gain_ref, w_ref = refs[8:10]
    send, kept, left = refs[-3:]
    x, c = lax.axis_index("x"), lax.axis_index("c")
    order = (x, around(x, 3), around(x, 1), around(x, 2))
    for k, ref in enumerate(refs[:8]):
        left[k // 4 * SPAN : k // 4 * SPAN + SPAN, lanes(order[k % 4], WIDTH)] = ref[...]
    plain = left[...] * (1.0 / gain_ref[...]).astype(BF16)
    ones = jnp.ones((NX * WIDTH, 128), BF16)
    mean = jnp.dot(plain * plain, ones, preferred_element_type=F32) * (1.0 / (NX * WIDTH))
    scale = lax.rsqrt(mean + 1e-05)
    scale = jnp.concatenate([scale, scale], axis=1)
    for core, out in ((1 - c, send), (c, kept)):
        for yy in range(0, NY, 2):
            w = jnp.concatenate([w_ref[2 * yy + core], w_ref[2 * yy + 2 + core]], axis=1)
            acc = jnp.dot(left[...], w, preferred_element_type=F32)
            acc = (acc * scale).astype(out.dtype)
            out[yy] = acc[:, :128]
            out[yy + 1] = acc[:, 128:]


def hold_kernel(w_any, after, out, sem):
    copy = pltpu.make_async_copy(w_any, out, sem)
    copy.start()
    copy.wait()


def cores_kernel(kept, got, to_next, to_prev, to_far, mine):
    y = lax.axis_index("y")
    for by, out in ((1, to_next), (3, to_prev), (2, to_far), (0, mine)):
        q = around(y, by)
        out[...] = (kept[q] + got[q].astype(F32)).astype(out.dtype)


def rows_kernel(a0, a1, a2, a3, b0, b1, b2, b3, own, to_next, to_prev, to_far, whole):
    x = lax.axis_index("x")
    first = a0[...] + a1[...].astype(F32) + a2[...].astype(F32) + a3[...].astype(F32)
    second = b0[...] + b1[...].astype(F32) + b2[...].astype(F32) + b3[...].astype(F32)
    whole[0] = first[:SPAN]
    whole[1] = first[SPAN:]
    whole[2] = second[:SPAN]
    whole[3] = second[SPAN:]
    for by, out in ((0, own), (1, to_next), (3, to_prev), (2, to_far)):
        out[...] = whole[around(x, by)].astype(BF16)


def place_kernel(own, prev, nxt, far, out):
    x = lax.axis_index("x")
    for by, got in ((0, own), (3, prev), (1, nxt), (2, far)):
        out[:, lanes(around(x, by), 128)] = got[...]


def on_device(
    x_in, bc_in, gate_in, dt_raw, decay_rate, skip_gain, conv_x, conv_bc, norm_gain, out_weight, lengths
):
    nz = lax.axis_size("z")
    w_all = lax.all_gather(out_weight, "z", axis=0)
    bc = bc_in.reshape(SPAN, BC)

    piece = ((SPAN + 16, BC), BF16)
    quarter = ((SPAN, WIDTH), BF16)
    edge = ((16, WIDE), BF16)
    packed = call(
        pack_kernel, "hhh", (x_in, bc, dt_raw.T), [piece] * 4 + [quarter] * 4 + [edge] * 4,
        [pltpu.VMEM((4 * HEADS, SPAN), F32), pltpu.SemaphoreType.DMA((17,))],
        nbytes=6 << 20,
    )

    def spread_out(to_next, to_prev, to_far, own):
        return own, shift(to_next, "x", 1), shift(to_prev, "x", -1), shift(to_far, "x", 2)

    def behind(v, k):
        return lax.ppermute(v, ("z", "x"), [((z - 1) * NX + NX - 1, z * NX + k) for z in range(1, nz)])

    bcs = spread_out(*packed[0:4])
    xs_in = spread_out(*packed[4:8])
    halo = [behind(e, k) for k, e in enumerate(packed[8:12])]
    far = xs_in[3]
    g_own, g_next, g_prev, g_far = call(
        split_kernel, "ha", (gate_in, far), [quarter] * 4, [pltpu.SemaphoreType.DMA((4,))],
        nbytes=2 << 20,
    )
    gates = (g_own, shift(g_next, "x", 1), shift(g_prev, "x", -1), shift(g_far, "x", 2))

    gain = norm_gain[None, :]
    rows = STATE // nz
    blocks_bc = pltpu.VMEM((NX, SPAN, BC), BF16)
    blocks_cols = pltpu.VMEM((NX, SPAN, 128), F32)
    blocks_rows = pltpu.VMEM((NX, 2 * HEADS, SPAN), F32)
    bcv, cols, lines, reach, total = call(
        step_kernel, "ss" + "v" * 9,
        (lengths, decay_rate, *halo, *bcs, conv_bc),
        [
            ((NX, SPAN, BC), BF16),
            ((NX, SPAN, 128), F32),
            ((NX, 2 * HEADS, SPAN), F32),
            ((NX, SPAN, 128), F32),
            ((8, 128), F32),
        ],
        [
            pltpu.VMEM((NX, SPAN + 16, BC), BF16),
            pltpu.VMEM((SPAN + 8, BC), F32),
            blocks_bc, blocks_cols, blocks_rows, blocks_cols,
            pltpu.SemaphoreType.DMA((4, NX)),
        ],
        flops=2 << 30, nbytes=8 << 20, places="hhhhv",
    )
    xs, carry, sums = call(
        state_kernel, "s" + "v" * 12,
        (lengths, *xs_in, *halo, conv_x, bcv, cols, total),
        [
            ((NX, SPAN, WIDTH), BF16),
            ((NX, STATE, WIDTH), BF16),
            ((nz, rows, WIDTH + 128), BF16),
        ],
        [
            pltpu.VMEM((NX, SPAN, WIDTH), BF16),
            pltpu.VMEM((SPAN + 8, WIDTH), F32),
            pltpu.VMEM((STATE, WIDTH), F32),
            pltpu.VMEM((SPAN, WIDTH), BF16),
            blocks_bc,
            blocks_bc,
            pltpu.SemaphoreType.DMA((2, NX)),
        ],
        flops=3 << 30, nbytes=10 << 20, places="hhv",
    )
    spread = lax.all_to_all(sums, "z", 0, 0, tiled=True)
    (mine,) = call(scan_kernel, "v", (spread,), [((nz, rows, WIDTH), BF16)], nbytes=1 << 20)
    (y_loc,) = call(
        within_kernel, "sshhhhhaaaa", (lengths, skip_gain, xs, bcv, cols, lines, carry, mine, *gates[1:]),
        [((NX, SPAN, WIDTH), F32)],
        [
            pltpu.VMEM((SPAN, SPAN), F32),
            blocks_bc, blocks_bc, blocks_cols, blocks_rows, blocks_bc,
            pltpu.VMEM((NX, SPAN, WIDTH), F32),
            pltpu.SemaphoreType.DMA((6, NX)),
        ],
        flops=6 << 30, nbytes=16 << 20, places="h",
    )
    enter = lax.all_to_all(mine, "z", 0, 0, tiled=True).reshape(STATE, WIDTH)

    halves = []
    v = call(
        gate_kernel, "aaaahhhava", (*gates, y_loc, bcv, reach, enter, gain, w_all),
        [quarter] * NX,
        [
            pltpu.VMEM((NX, SPAN, WIDTH), BF16),
            pltpu.VMEM((NX, SPAN, WIDTH), F32),
            pltpu.VMEM((NX, SPAN, STATE), BF16),
            pltpu.VMEM((NX, SPAN, 128), F32),
            pltpu.VMEM((STATE, WIDTH), BF16),
            pltpu.SemaphoreType.DMA((17,)),
        ],
        flops=2 << 30, nbytes=6 << 20,
    )
    parts = []
    for k, o in enumerate(v):
        a, b = shift(o, "x", 1), shift(o, "x", -1)
        parts += [o, a, b, shift(a, "x", 1) if k % 2 == 0 else shift(b, "x", -1)]
    gathered = (parts[:8], parts[8:])
    (w_near,) = call(
        hold_kernel, "aa", (w_all, v[-1]), [((nz, NX * WIDTH, 128), BF16)],
        [pltpu.SemaphoreType.DMA(())], nbytes=1 << 20, vmem=SMALL,
    )
    after = tuple(parts[k] for k in (9, 10, 11, 13, 14, 15))
    for parts in gathered:
        send, kept = call(
            product_kernel, "v" * 10 + "a" * len(after), (*parts, gain, w_near, *after),
            [((NY, 2 * SPAN, 128), BF16), ((NY, 2 * SPAN, 128), F32)],
            [
                pltpu.VMEM((2 * SPAN, NX * WIDTH), BF16),
            ],
            flops=3 << 30, nbytes=8 << 20, vmem=SMALL,
        )
        got = shift(send, "c", 1)
        part = ((2 * SPAN, 128), BF16)
        y_next, y_prev, y_far, mine = call(
            cores_kernel, "vv", (kept, got), [part] * 3 + [((2 * SPAN, 128), F32)], nbytes=2 << 20, vmem=SMALL
        )
        after = ()
        halves += [mine, shift(y_next, "y", 1), shift(y_prev, "y", -1), shift(y_far, "y", 2)]
    tile = ((SPAN, 128), BF16)
    own, to_next, to_prev, to_far = call(
        rows_kernel, "v" * 8, halves, [tile] * 4, [pltpu.VMEM((NX, SPAN, 128), F32)], nbytes=2 << 20, vmem=SMALL
    )
    (mixed,) = call(
        place_kernel, "vvvv",
        (own, shift(to_next, "x", 1), shift(to_prev, "x", -1), shift(to_far, "x", 2)),
        [((SPAN, NX * 128), BF16)], nbytes=1 << 20, vmem=SMALL,
    )
    return mixed


def solution(mesh):
    seq, tp = ("z", "x"), ("y", "c")
    fine = Mesh(mesh.devices.reshape(mesh.devices.shape[0] // NX, NX, NY, 2), seq + tp)
    in_specs = (
        P(seq, tp),
        P(seq, tp, None),
        P(seq, tp),
        P(seq, tp),
        P(tp),
        P(tp),
        P(None, tp),
        P(None, tp, None),
        P(tp),
        P(tp, seq),
        P(),
    )
    return jax.shard_map(
        on_device, mesh=fine, in_specs=in_specs, out_specs=P(seq, tp), check_vma=False
    )
```
